512 devices in a mesh: dp: 32 (over z, y_lo), fsdp: 16 (over x, y_hi, core).
Axes of the slice: x: 4, y: 4 (y_hi: 2, y_lo: 2; y = y_hi * 2 + y_lo), z: 16, core: 2. Of those that a mesh axis runs over, the one named last changes fastest.
Arguments:
- hidden: bfloat16 [8192, 2048], P('dp', 'fsdp'), may hold values from -6 to 6
- upstream: bfloat16 [8192, 16384], P('dp', 'fsdp'), may hold values from -6 to 6
- rewards: float32 [256], P('dp'), may hold values from -4 to 4
- groups: int32 [256], P('dp'), may hold values from 0 to 63, as said below
- lengths: int32 [256], P('dp'), may hold values from 1 to 32, 6144 in all
- frozen_projection_weight: bfloat16 [2048, 16384], P('dp', 'fsdp'), may hold values from -0.125 to 0.125
- adapter_down_factor: float32 [256, 2048], P('dp', 'fsdp'), may hold values from -0.125 to 0.125
- adapter_up_factor: float32 [256, 16384], P('dp', 'fsdp'), may hold values from -0.01953125 to 0.01953125
- down_first_moment: float32 [256, 2048], P('dp', 'fsdp'), may hold values from -48.87522 to 48.87522
- down_second_moment: float32 [256, 2048], P('dp', 'fsdp'), may hold values from 0.8912896 to 8.912896
- up_first_moment: float32 [256, 16384], P('dp', 'fsdp'), may hold values from -122.18805 to 122.18805
- up_second_moment: float32 [256, 16384], P('dp', 'fsdp'), may hold values from 5.48864 to 54.8864
Outputs:
- hidden_input_gradient: bfloat16 [8192, 2048], P('dp', 'fsdp')
- fresh_down_factor: float32 [256, 2048], P('dp', 'fsdp')
- fresh_up_factor: float32 [256, 16384], P('dp', 'fsdp')
- fresh_down_first_moment: float32 [256, 2048], P('dp', 'fsdp')
- fresh_down_second_moment: float32 [256, 2048], P('dp', 'fsdp')
- fresh_up_first_moment: float32 [256, 16384], P('dp', 'fsdp')
- fresh_up_second_moment: float32 [256, 16384], P('dp', 'fsdp')
- sampler_merged_weight: bfloat16 [2048, 16384], P(None, 'fsdp')
The draws below stay inside these ranges and needn't reach their ends.
Inputs may be any that keep to these rules, and one draw needn't show every extreme that they name: `groups`: each group holds exactly 4 completions, and all completions of a group lie in one aligned block of 8 completions.
All inputs are finite; a program needn't handle non-finite values. No bound on the sum of `lengths` on one device may be relied on, other than what follows from the above.
Results may differ from the reference program's by a relative error of at most 0.0051.
Values may be sent and summed in bfloat16 or wider, within the bound.
A program may use at most 64 MiB of HBM per device.

```python
import math
import jax
import jax.numpy as jnp
import numpy as np
from jax import lax

MODEL_WIDTH = 16384
HIDDEN_SLICE = 2048
ADAPTER_RANK = 256
GROUP = 4
LEN = 32
SEQ_DEV = 8
SEQS = 256
TOKENS = 8192


def draw_groups(key, part):
    key = jax.random.fold_in(key, 11)
    blocks = SEQS // SEQ_DEV
    keys = jax.random.split(key, blocks)
    orders = jax.vmap(lambda one_key: jax.random.permutation(one_key, SEQ_DEV))(keys)
    offsets = jnp.arange(blocks, dtype=jnp.int32)[:, None] * (SEQ_DEV // GROUP)
    labels = orders.astype(jnp.int32) // GROUP + offsets
    return labels.reshape(SEQS).astype(jnp.int32)


def block_scale(stream_key, extent, pieces, least, largest):
    loudness, own = 1.0, jax.random.fold_in(stream_key, 6)
    for dim, shards_of in pieces:
        steps = jnp.exp(jax.random.uniform(jax.random.fold_in(own, dim), (shards_of,), jnp.float32, least / len(pieces), largest / len(pieces)))
        loudness = loudness * jnp.repeat(steps, extent[dim] // shards_of).reshape([-1 if axis == dim else 1 for axis in range(len(extent))])
    return loudness


def profile(number_of, total, bound, slope):
    loads = [(1 << 20) // math.isqrt(rank ** slope) + 1 for rank in range(2, number_of + 1)]
    spare, given = total - bound - (number_of - 1), [1] * (number_of - 1)
    while spare > 0:
        free = [i for i in range(number_of - 1) if given[i] < bound]
        mass, budget = sum([loads[i] for i in free]), spare
        for i in free:
            more = min(bound - given[i], max(1, budget * loads[i] // mass), spare)
            given[i] = given[i] + more
            spare = spare - more
    return np.array([bound] + given)


def uneven_parts(own_key, count, total, limit, slope):
    if count == 2:
        one = jax.random.randint(own_key, (), max(1, total - limit), min(limit, total - 1) + 1)
        return jnp.stack([one, total - one])
    sizes = jnp.asarray(profile(count, total, limit, slope), jnp.int32)
    twos = (count - 1) // 2
    donor, taker = sizes[1:1 + 2 * twos:2], sizes[2:2 + 2 * twos:2]
    slack = jnp.minimum(donor - 1, limit - taker)
    moved = jax.random.randint(jax.random.fold_in(own_key, 1), (twos,), 0, 1 << 20) % (slack + 1)
    sizes = sizes.at[1:1 + 2 * twos:2].set(donor - moved).at[2:2 + 2 * twos:2].set(taker + moved)
    return sizes[jax.random.permutation(jax.random.fold_in(own_key, 2), count)]


def bell_draw(own_key, shape, width, bound, cuts=(), kind=jnp.bfloat16):
    entries = jax.random.normal(own_key, shape, jnp.float32) * width
    if len(cuts) > 0:
        entries = block_scale(own_key, shape, cuts, -0.22, 0.18) * entries
    return jnp.clip(entries, min=-bound, max=bound).astype(kind)


def setup_inputs(seed: int = 0) -> dict:
    streams_of = jax.random.split(jax.random.key(seed), 13)
    hidden = bell_draw(streams_of[0], (TOKENS, HIDDEN_SLICE), 1.0, 6.0, ((0, 32), (1, 16)))
    upstream = bell_draw(streams_of[1], (TOKENS, MODEL_WIDTH), 1.0, 6.0, ((0, 32), (1, 16)))
    rewards = bell_draw(streams_of[2], (SEQS,), 1.0, 4.0, ((0, 32),), jnp.float32)
    groups = draw_groups(jax.random.fold_in(streams_of[12], 71), 0)
    lengths = uneven_parts(streams_of[4], SEQS, SEQS * LEN * 3 // 4, LEN, 0).astype(jnp.int32)
    frozen_projection_weight = bell_draw(streams_of[5], (HIDDEN_SLICE, MODEL_WIDTH), HIDDEN_SLICE ** -0.5, 0.125, ((0, 32), (1, 16)))
    adapter_down_factor = bell_draw(streams_of[6], (ADAPTER_RANK, HIDDEN_SLICE), HIDDEN_SLICE ** -0.5, 0.125, ((0, 32), (1, 16)), jnp.float32)
    adapter_up_factor = bell_draw(streams_of[7], (ADAPTER_RANK, MODEL_WIDTH), (400 * ADAPTER_RANK) ** -0.5, 0.01953125, ((0, 32), (1, 16)), jnp.float32)
    down_first_moment = bell_draw(streams_of[8], (ADAPTER_RANK, HIDDEN_SLICE), (0.0225 * (TOKENS * MODEL_WIDTH // ADAPTER_RANK) ** 0.5), 48.87522, ((0, 32), (1, 16)), jnp.float32)
    down_second_moment = jnp.clip(jnp.exp(math.log(8.912896) - 2.3025851 * jax.random.uniform(streams_of[9], (ADAPTER_RANK, HIDDEN_SLICE), jnp.float32) ** block_scale(streams_of[9], (ADAPTER_RANK, HIDDEN_SLICE), ((0, 32), (1, 16)), -0.2, 0.2)), 0.8912896, 8.912896)
    up_first_moment = bell_draw(streams_of[10], (ADAPTER_RANK, MODEL_WIDTH), (0.45 * TOKENS ** 0.5), 122.18805, ((0, 32), (1, 16)), jnp.float32)
    up_second_moment = jnp.clip(jnp.exp(math.log(54.8864) - 2.3025851 * jax.random.uniform(streams_of[11], (ADAPTER_RANK, MODEL_WIDTH), jnp.float32) ** block_scale(streams_of[11], (ADAPTER_RANK, MODEL_WIDTH), ((0, 32), (1, 16)), -0.2, 0.2)), 5.48864, 54.8864)
    return {"hidden": hidden, "upstream": upstream, "rewards": rewards, "groups": groups, "lengths": lengths, "frozen_projection_weight": frozen_projection_weight, "adapter_down_factor": adapter_down_factor, "adapter_up_factor": adapter_up_factor, "down_first_moment": down_first_moment, "down_second_moment": down_second_moment, "up_first_moment": up_first_moment, "up_second_moment": up_second_moment}


adapter_scale = 2.0
learn_rate = 0.003
beta_one = 0.9
beta_two = 0.999
corr_one = 1.0 - 0.9 ** 10
corr_two = 1.0 - 0.999 ** 10
adam_eps = 1e-08

def optimizer_update(param, grad, mean, var):
    next_mean = beta_one * mean + (1.0 - beta_one) * grad
    next_var = beta_two * var + (1.0 - beta_two) * grad * grad
    update = next_mean / corr_one / (jnp.sqrt(next_var / corr_two) + adam_eps)
    return (param - learn_rate * update, next_mean, next_var)

def reference(hidden, upstream, rewards, groups, lengths, frozen_projection_weight, adapter_down_factor, adapter_up_factor, down_first_moment, down_second_moment, up_first_moment, up_second_moment):
    same = groups[:, None] == groups[None, :]
    group_mean = lax.optimization_barrier(jnp.sum(jnp.where(same, rewards[None, :], jnp.float32(0.0)), axis=1)) / GROUP
    advantage = rewards - group_mean
    positions = jnp.arange(LEN, dtype=jnp.int32)
    valid = positions[None, :] < lengths[:, None]
    weight = jnp.where(valid, -advantage[:, None], jnp.float32(0.0)).reshape(TOKENS)
    output_gradient = (weight[:, None] * upstream.astype(jnp.float32)).astype(jnp.bfloat16)
    down_factor_portion = adapter_down_factor.astype(jnp.bfloat16)
    up_factor_portion = adapter_up_factor.astype(jnp.bfloat16)
    reduced_input = jnp.dot(hidden, down_factor_portion.T, preferred_element_type=jnp.float32).astype(jnp.bfloat16)
    reduced_output = jnp.dot(output_gradient, up_factor_portion.T, preferred_element_type=jnp.float32).astype(jnp.bfloat16)
    up_factor_gradient = adapter_scale * jnp.dot(reduced_input.T, output_gradient, preferred_element_type=jnp.float32)
    down_factor_gradient = adapter_scale * jnp.dot(reduced_output.T, hidden, preferred_element_type=jnp.float32)
    frozen_contribution = jnp.dot(output_gradient, frozen_projection_weight.T, preferred_element_type=jnp.float32)
    adapter_contribution = jnp.dot(reduced_output, down_factor_portion, preferred_element_type=jnp.float32)
    hidden_input_gradient = (frozen_contribution + adapter_scale * adapter_contribution).astype(jnp.bfloat16)
    fresh_down_factor, fresh_down_first_moment, fresh_down_second_moment = optimizer_update(adapter_down_factor, down_factor_gradient, down_first_moment, down_second_moment)
    fresh_up_factor, fresh_up_first_moment, fresh_up_second_moment = optimizer_update(adapter_up_factor, up_factor_gradient, up_first_moment, up_second_moment)
    down_next_half = fresh_down_factor.astype(jnp.bfloat16)
    up_next_half = fresh_up_factor.astype(jnp.bfloat16)
    weight_delta = jnp.dot(down_next_half.T, up_next_half, preferred_element_type=jnp.float32)
    sampler_merged_weight = (frozen_projection_weight.astype(jnp.float32) + adapter_scale * weight_delta).astype(jnp.bfloat16)
    return (hidden_input_gradient, fresh_down_factor, fresh_up_factor, fresh_down_first_moment, fresh_down_second_moment, fresh_up_first_moment, fresh_up_second_moment, sampler_merged_weight)
```

```python
import jax
import jax.numpy as jnp
from jax import lax
from jax.experimental import pallas as pl
from jax.experimental.pallas import tpu as pltpu
from jax.sharding import PartitionSpec as P

GROUP = 4
LEN = 32
MESH = pl.DeviceIdType.MESH

adapter_scale = 2.0
learn_rate = 0.003
beta_one = 0.9
beta_two = 0.999
corr_one = 1.0 - 0.9**10
corr_two = 1.0 - 0.999**10
adam_eps = 1e-08

bf16 = jnp.bfloat16
f32 = jnp.float32

Y_LO = (0, 1, 0, 0, 0)
Y_HI = (0, 0, 0, 1, 0)
CORE = (0, 0, 0, 0, 1)
FAR = tuple((dz, 0, 0, 0, 0) for dz in (8, 4, -4))
NEAR = tuple((dz, 0, 0, 0, 0) for dz in (2, 1, -1))
X_RING = tuple((0, 0, dx, 0, 0) for dx in (2, 1, -1))
X_CORE = tuple((0, 0, dx, 0, dc) for dx in (2, 1, -1, 0) for dc in (1, 0) if (dx, dc) != (0, 0))
PEERS = FAR + NEAR + (Y_LO, Y_HI) + X_CORE


def coords():
    dp = lax.axis_index("dp")
    fs = lax.axis_index("fsdp")
    return dp // 2, dp % 2, fs // 4, (fs // 2) % 2, fs % 2


def device(off):
    z, yl, x, yh, c = coords()
    z = (z + off[0] + 16) % 16
    yl = (yl + off[1]) % 2
    x = (x + off[2] + 4) % 4
    yh = (yh + off[3]) % 2
    c = (c + off[4]) % 2
    return (2 * z + yl, 4 * x + 2 * yh + c)


def inverse(off):
    return (-off[0], off[1], -off[2], off[3], off[4])


def dot(left, right, left_dim, right_dim):
    return lax.dot_general(
        left, right, (((left_dim,), (right_dim,)), ((), ())), preferred_element_type=f32
    )


def rows(start, size):
    return pl.ds(pl.multiple_of(start * size, size), size)


def adam(param, grad, mean, var):
    next_mean = beta_one * mean + (1.0 - beta_one) * grad
    next_var = beta_two * var + (1.0 - beta_two) * grad * grad
    update = next_mean / corr_one / (jnp.sqrt(next_var / corr_two) + adam_eps)
    return (param - learn_rate * update, next_mean, next_var)


def exchange_kernel(
    hid, ups, wt, w_own, dn, up, dm, dv, um, uv,
    w_all, nd, fu, hig, fdn, fup, fdm, fdv, fum, fuv,
    g, wb, pair, f, a, rx, sy, ty, low,
    cd, cu, nrd, nru, md, mu, frd, fru, yd, yu, yrd, yru, pd, pu, fd,
    pt, pr1, q, pr2, r, rb, pr3, send_sem, recv_sem, local_sem,
):
    z, yl, x, yh, c = coords()
    pos = (z % 4) * 4 + z // 4
    count = [0]
    sent = []

    def send(src, dst, off):
        i = count[0]
        assert i < 72
        count[0] += 1
        copy = pltpu.make_async_remote_copy(
            src_ref=src,
            dst_ref=dst,
            send_sem=send_sem.at[i],
            recv_sem=recv_sem.at[i],
            device_id=device(off),
            device_id_type=MESH,
        )
        copy.start()
        sent.append(copy)
        return copy

    def arrive(copies):
        for copy in copies:
            copy.wait_recv()

    def pair_send(buf):
        return send(buf.at[rows(yl, 8)], buf.at[rows(yl, 8)], Y_LO)

    def far_send(buf):
        mine = rows(pos, 16)
        return [send(buf.at[mine], buf.at[mine], off) for off in FAR]

    def near_send(buf):
        mine = rows(z % 4, 64)
        return [send(buf.at[mine], buf.at[mine], off) for off in NEAR]

    def near_parts(buf, slots):
        return [
            send(buf.at[rows((z + off[0] + 16) % 4, 64)], slots.at[i], off)
            for i, off in enumerate(NEAR)
        ]

    def near_sum(buf, slots):
        total = buf[rows(z % 4, 64), :].astype(f32)
        for i in range(3):
            total = total + slots[i].astype(f32)
        return total

    def far_parts(buf, slots):
        return [
            send(buf.at[rows(((z + off[0] + 16) % 16) // 4, 16)], slots.at[i], off)
            for i, off in enumerate(FAR)
        ]

    def far_sum(buf, slots):
        total = buf[rows(z // 4, 16), :].astype(f32)
        for i in range(3):
            total = total + slots[i].astype(f32)
        return total

    def pair_parts(buf, slot):
        return send(buf.at[rows(1 - yl, 8)], slot, Y_LO)

    def w_group(group):
        return wb.at[rows(group % 4, 4), rows(yl, 64), :]

    def w_block(zz):
        zz = (zz + 16) % 16
        return wb.at[(zz % 4) * 4 + zz // 4, rows(yl, 64), :]

    barrier = pltpu.get_barrier_semaphore()
    for off in PEERS:
        pl.semaphore_signal(barrier, inc=1, device_id=device(inverse(off)), device_id_type=MESH)
    pair[rows(yl, 8), 0:1024] = up[...]
    pair[rows(yl, 8), 1024:1152] = dn[...]
    wb[pos, rows(yl, 64), :] = w_own[...]
    pl.semaphore_wait(barrier, len(PEERS))

    s = pair_send(pair)
    g[...] = (wt[...] * ups[...].astype(f32)).astype(bf16)
    s.wait_recv()
    f[rows(pos, 16), :] = pair[...].astype(bf16)
    far = far_send(f)
    w_far = [send(w_block(z), w_block(z), FAR[1]), send(w_block(z), w_block(z), FAR[2])]
    arrive(far)
    near = near_send(f)
    arrive(near)

    a[0:256, :] = dot(f[:, 1024:1152], hid[...], 1, 1).astype(bf16)
    a[256:512, :] = dot(f[:, 0:1024], g[...], 1, 1).astype(bf16)
    j = 2 * x + c
    scattered = []
    for i, off in enumerate(X_CORE):
        to = 2 * ((x + off[2] + 4) % 4) + (c + off[4]) % 2
        scattered.append(send(a.at[rows(to, 64)], rx.at[i], off))
    arrive(w_far)
    w_far2 = send(w_block(z - 4), w_block(z - 4), FAR[1])
    arrive(scattered)
    total = a[rows(j, 64), :].astype(f32)
    for i in range(7):
        total = total + rx[i].astype(f32)
    sy[...] = total.astype(bf16)
    s = send(sy, ty, Y_HI)
    s.wait_recv()
    low[rows(j, 64), :] = (sy[...].astype(f32) + ty[...].astype(f32)).astype(bf16)
    gathered = [send(low.at[rows(j, 64)], low.at[rows(j, 64)], off) for off in X_CORE]
    w_far2.wait_recv()
    w_near = [send(w_group(z), w_group(z), NEAR[1]), send(w_group(z), w_group(z), NEAR[2])]
    w_pair = [send(w_group(z), w_group(z), Y_LO)]
    arrive(gathered)

    cd[...] = (adapter_scale * dot(low[256:512, :], hid[...], 1, 0)).astype(bf16)
    near_d = near_parts(cd, nrd)
    cu[...] = (adapter_scale * dot(low[0:256, :], g[...], 1, 0)).astype(bf16)
    near_u = near_parts(cu, nru)
    arrive(near_d)
    md[...] = near_sum(cd, nrd).astype(bf16)
    far_d = far_parts(md, frd)
    arrive(near_u)
    mu[...] = near_sum(cu, nru).astype(bf16)
    far_u = far_parts(mu, fru)
    arrive(w_near)
    w_near2 = send(w_group(z + 1), w_group(z + 1), NEAR[2])
    w_pair.append(send(w_group(z + 1), w_group(z + 1), Y_LO))
    w_pair.append(send(w_group(z + 3), w_group(z + 3), Y_LO))
    arrive(far_d)
    yd[...] = far_sum(md, frd)
    s = pair_parts(yd, yrd)
    s.wait_recv()
    fdn[...], fdm[...], fdv[...] = adam(dn[...], yd[rows(yl, 8), :] + yrd[...], dm[...], dv[...])
    pd[rows(yl, 8), :] = fdn[...]
    s = pair_send(pd)
    arrive(far_u)
    yu[...] = far_sum(mu, fru)
    s_u = pair_parts(yu, yru)
    s.wait_recv()
    fd[rows(pos, 16), :] = pd[...].astype(bf16)
    far_d = far_send(fd)
    s_u.wait_recv()
    fup[...], fum[...], fuv[...] = adam(up[...], yu[rows(yl, 8), :] + yru[...], um[...], uv[...])
    pu[rows(yl, 8), :] = fup[...]
    s_u = pair_send(pu)
    w_near2.wait_recv()
    w_pair.append(send(w_group(z + 2), w_group(z + 2), Y_LO))
    s_u.wait_recv()
    fu[rows(pos, 16), :] = pu[...].astype(bf16)
    far_u = far_send(fu)
    arrive(far_d)
    near_d = near_send(fd)
    arrive(far_u)
    near_u = near_send(fu)
    arrive(near_d)

    k = 2 * x + yh
    nd[c, k] = fd[...]
    s = send(nd.at[c, k], nd.at[c, k], Y_HI)

    arrive(w_pair)
    w_copy = pltpu.make_async_copy(wb, w_all, local_sem)
    w_copy.start()

    def product(p, carry):
        group = p // 4
        pt[group % 2, 2 * (p % 4) + group // 2] = dot(wb[p], g[...], 1, 1).astype(bf16)
        return carry

    lax.fori_loop(0, 16, product, 0)
    s_p = send(pt.at[1 - c], pr1, CORE)
    s.wait_recv()
    spread = [send(nd.at[c, rows(x, 2)], nd.at[c, rows(x, 2)], off) for off in X_RING]
    s_p.wait_recv()

    def core_sum(i, carry):
        q[i] = (pt[c, i].astype(f32) + pr1[i].astype(f32)).astype(bf16)
        return carry

    lax.fori_loop(0, 8, core_sum, 0)
    x_parts = [
        send(q.at[rows((x + off[2] + 4) % 4, 2)], pr2.at[i], off) for i, off in enumerate(X_RING)
    ]
    arrive(spread)
    s = send(nd.at[c], nd.at[c], CORE)
    arrive(x_parts)
    total = q[rows(x, 2)].astype(f32)
    for i in range(3):
        total = total + pr2[i].astype(f32)
    r[...] = total
    rb[...] = r[1 - yh].astype(bf16)
    s_p = send(rb, pr3, Y_HI)
    own = adapter_scale * dot(low[256:512, :], f[:, 1024:1152], 0, 0)
    s_p.wait_recv()
    hig[...] = (jnp.transpose(r[yh] + pr3[...].astype(f32)) + own).astype(bf16)
    s.wait_recv()
    arrive(near_u)
    for copy in sent:
        copy.wait_send()
    w_copy.wait()


def exchange(*args):
    def out(shape, dtype):
        return jax.ShapeDtypeStruct(shape, dtype)

    vmem = pl.BlockSpec(memory_space=pltpu.VMEM)
    scratch = [
        ((256, 1024), bf16), ((16, 128, 1024), bf16), ((16, 1152), f32), ((256, 1152), bf16),
        ((512, 256), bf16), ((7, 64, 256), bf16), ((64, 256), bf16), ((64, 256), bf16),
        ((512, 256), bf16),
        ((256, 128), bf16), ((256, 1024), bf16), ((3, 64, 128), bf16), ((3, 64, 1024), bf16),
        ((64, 128), bf16), ((64, 1024), bf16), ((3, 16, 128), bf16), ((3, 16, 1024), bf16),
        ((16, 128), f32), ((16, 1024), f32), ((8, 128), f32), ((8, 1024), f32),
        ((16, 128), f32), ((16, 1024), f32), ((256, 128), bf16),
        ((2, 8, 128, 256), bf16), ((8, 128, 256), bf16), ((8, 128, 256), bf16),
        ((3, 2, 128, 256), bf16), ((2, 128, 256), f32), ((128, 256), bf16), ((128, 256), bf16),
    ]
    messages = 72
    return pl.pallas_call(
        exchange_kernel,
        name="exchange",
        out_shape=[
            out((16, 128, 1024), bf16),
            out((2, 8, 256, 128), bf16),
            out((256, 1024), bf16),
            out((256, 128), bf16),
            out((8, 128), f32),
            out((8, 1024), f32),
            out((8, 128), f32),
            out((8, 128), f32),
            out((8, 1024), f32),
            out((8, 1024), f32),
        ],
        in_specs=[vmem] * 10,
        out_specs=[pl.BlockSpec(memory_space=pl.ANY)] + [vmem] * 9,
        scratch_shapes=[pltpu.VMEM(shape, dtype) for shape, dtype in scratch]
        + [
            pltpu.SemaphoreType.DMA((messages,)),
            pltpu.SemaphoreType.DMA((messages,)),
            pltpu.SemaphoreType.DMA,
        ],
        compiler_params=pltpu.CompilerParams(
            collective_id=0, has_side_effects=True, vmem_limit_bytes=40 << 20
        ),
    )(*args)


def merge_kernel(w, nd, fu, *refs):
    merged = refs[-1]
    merged[...] = (
        w[0].astype(f32) + adapter_scale * dot(nd[0, 0], fu[...], 0, 0)
    ).astype(bf16)

    @pl.when(pl.program_id(0) == 0)
    def _():
        for i in range(7):
            refs[7 + i][...] = refs[i][...]


def merge(w, nd, fu, *rest):
    def whole(array):
        return pl.BlockSpec(array.shape, lambda i: (0,) * len(array.shape))

    return pl.pallas_call(
        merge_kernel,
        name="merge",
        grid=(16,),
        in_specs=[
            pl.BlockSpec((1, 128, 1024), lambda i: ((i % 4) * 4 + i // 4, 0, 0)),
            pl.BlockSpec((1, 1, 256, 128), lambda i: (i % 2, 2 * (i // 4) + (i // 2) % 2, 0, 0)),
            whole(fu),
        ]
        + [whole(array) for array in rest],
        out_specs=[whole(array) for array in rest]
        + [pl.BlockSpec((128, 1024), lambda i: (i, 0))],
        out_shape=[jax.ShapeDtypeStruct(array.shape, array.dtype) for array in rest]
        + [jax.ShapeDtypeStruct((2048, 1024), bf16)],
        compiler_params=pltpu.CompilerParams(vmem_limit_bytes=40 << 20),
    )(w, nd, fu, *rest)


def body(
    hidden,
    upstream,
    rewards,
    groups,
    lengths,
    frozen_projection_weight,
    adapter_down_factor,
    adapter_up_factor,
    down_first_moment,
    down_second_moment,
    up_first_moment,
    up_second_moment,
):
    same = groups[:, None] == groups[None, :]
    group_mean = jnp.sum(jnp.where(same, rewards[None, :], jnp.float32(0.0)), axis=1) / GROUP
    advantage = rewards - group_mean
    positions = jnp.arange(LEN, dtype=jnp.int32)
    valid = positions[None, :] < lengths[:, None]
    weight = jnp.where(valid, -advantage[:, None], jnp.float32(0.0)).reshape(hidden.shape[0], 1)
    w_all, nd, fu, *rest = exchange(
        hidden,
        upstream,
        weight,
        frozen_projection_weight,
        adapter_down_factor,
        adapter_up_factor,
        down_first_moment,
        down_second_moment,
        up_first_moment,
        up_second_moment,
    )
    return tuple(merge(w_all, nd, fu, *rest))


def solution(mesh):
    split = P("dp", "fsdp")
    in_specs = (split, split, P("dp"), P("dp"), P("dp")) + (split,) * 7
    out_specs = (split,) * 7 + (P(None, "fsdp"),)
    return jax.shard_map(body, mesh=mesh, in_specs=in_specs, out_specs=out_specs, check_vma=False)
```

```python
import jax
import jax.numpy as jnp
from jax import lax
from jax.experimental import pallas as pl
from jax.experimental.pallas import tpu as pltpu
from jax.sharding import PartitionSpec as P

GROUP = 4
LEN = 32
MESH = pl.DeviceIdType.MESH

adapter_scale = 2.0
learn_rate = 0.003
beta_one = 0.9
beta_two = 0.999
corr_one = 1.0 - 0.9**10
corr_two = 1.0 - 0.999**10
adam_eps = 1e-08

bf16 = jnp.bfloat16
f32 = jnp.float32

Y_LO = (0, 1, 0, 0, 0)
Y_HI = (0, 0, 0, 1, 0)
CORE = (0, 0, 0, 0, 1)
FAR = tuple((dz, dy, 0, 0, 0) for dz, dy in ((4, 0), (-4, 1), (4, 1), (-4, 0), (0, 1)))
PLUS4, MINUS4_ACROSS, _, MINUS4, _ = FAR
NEAR = tuple((dz, 0, 0, 0, 0) for dz in (2, -2, 1, -1))
PLUS2, MINUS2, PLUS1, MINUS1 = NEAR
X_RING = tuple((0, 0, dx, 0, 0) for dx in (2, 1, -1))
X_CORE = tuple((0, 0, dx, 0, dc) for dx in (2, 1, -1, 0) for dc in (1, 0) if (dx, dc) != (0, 0))
PEERS = FAR + NEAR + (Y_HI,) + X_CORE
MESSAGES = 128


def coords():
    dp = lax.axis_index("dp")
    fs = lax.axis_index("fsdp")
    return dp // 2, dp % 2, fs // 4, (fs // 2) % 2, fs % 2


def device(off):
    z, yl, x, yh, c = coords()
    z = (z + off[0] + 16) % 16
    yl = (yl + off[1]) % 2
    x = (x + off[2] + 4) % 4
    yh = (yh + off[3]) % 2
    c = (c + off[4]) % 2
    return (2 * z + yl, 4 * x + 2 * yh + c)


def inverse(off):
    return (-off[0], off[1], -off[2], off[3], off[4])


def dot(left, right, left_dim, right_dim):
    return lax.dot_general(
        left, right, (((left_dim,), (right_dim,)), ((), ())), preferred_element_type=f32
    )


def rows(start, size):
    return pl.ds(pl.multiple_of(start * size, size), size)


def adam(param, grad, mean, var):
    next_mean = beta_one * mean + (1.0 - beta_one) * grad
    next_var = beta_two * var + (1.0 - beta_two) * grad * grad
    update = next_mean / corr_one / (jnp.sqrt(next_var / corr_two) + adam_eps)
    return (param - learn_rate * update, next_mean, next_var)


def spread_columns(slot):
    return jnp.concatenate([slot[0:8], slot[8:16]], axis=1)


def stack_columns(block):
    half = block.shape[1] // 2
    return jnp.concatenate([block[:, :half], block[:, half:]], axis=0)


def exchange_kernel(
    rewards, groups, lengths, hid_in, ups_in, w_in, dn_in, up_in, dm_in, dv_in, um_in, uv_in,
    wb, nd, fu, hig, fdn, fup, fdm, fdv, fum, fuv,
    hid, ups, dn, up, dm, dv, um, uv,
    g, gt, sa, f, a, rx, sy, ty, low,
    cd, cu, nrd, nru, md, mu, frd, fru, hd, hu, sd, su, fd,
    pt, pr1, q, pr2, r, rb, pr3, send_sem, recv_sem, local_sem,
):
    z, yl, x, yh, c = coords()
    slot = 2 * (z // 4) + yl
    count = [0]
    sent = []

    def send(src, dst, off):
        i = count[0]
        count[0] += 1
        assert i < MESSAGES
        copy = pltpu.make_async_remote_copy(
            src_ref=src,
            dst_ref=dst,
            send_sem=send_sem.at[i],
            recv_sem=recv_sem.at[i],
            device_id=device(off),
            device_id_type=MESH,
        )
        copy.start()
        sent.append(copy)
        return copy

    def arrive(copies):
        for copy in copies:
            copy.wait_recv()

    def slot_of(dz, dy):
        return 2 * (((z + dz + 16) % 16) // 4) + (yl + dy) % 2

    def far_send(buf):
        return [send(buf.at[slot], buf.at[slot], off) for off in FAR]

    def far_relay(buf, copies):
        arrive(copies[:2])
        back, ahead = buf.at[slot_of(-4, 0)], buf.at[slot_of(4, 1)]
        return copies[2:] + [send(back, back, PLUS4), send(ahead, ahead, MINUS4)]

    def near_send(buf):
        mine = rows(z % 4, 64)
        low_half, high_half = rows(2 * (z % 4), 32), rows(2 * (z % 4) + 1, 32)
        return [
            send(buf.at[low_half], buf.at[low_half], PLUS2),
            send(buf.at[high_half], buf.at[high_half], MINUS2),
            send(buf.at[mine], buf.at[mine], PLUS1),
            send(buf.at[mine], buf.at[mine], MINUS1),
        ]

    def near_parts(buf, slots):
        across = (z + 2) % 4
        return [
            send(buf.at[rows(2 * across, 32)], slots.at[2, pl.ds(0, 32)], PLUS2),
            send(buf.at[rows(2 * across + 1, 32)], slots.at[2, pl.ds(32, 32)], MINUS2),
            send(buf.at[rows((z + 1) % 4, 64)], slots.at[0], PLUS1),
            send(buf.at[rows((z + 3) % 4, 64)], slots.at[1], MINUS1),
        ]

    def near_sum(buf, slots):
        total = buf[rows(z % 4, 64), :].astype(f32)
        for i in range(3):
            total = total + slots[i].astype(f32)
        return total

    def far_parts(buf, slots):
        relayed = [
            send(buf.at[slot_of(8, 0)], slots.at[5], PLUS4),
            send(buf.at[slot_of(8, 1)], slots.at[6], MINUS4),
        ]
        direct = [
            send(buf.at[slot_of(off[0], off[1])], slots.at[i], off)
            for i, off in enumerate(FAR)
            if i >= 2
        ]
        return relayed, direct

    def relay_parts(buf, slots, held, copies):
        relayed, direct = copies
        for i, off in enumerate(FAR[:2]):
            relayed[i].wait_recv()
            total = buf[slot_of(off[0], off[1])].astype(f32) + slots[5 + i].astype(f32)
            held[i] = total.astype(held.dtype)
            direct.append(send(held.at[i], slots.at[i], off))
        return direct

    def far_sum(buf, slots):
        total = buf[slot].astype(f32)
        for i in range(5):
            total = total + slots[i].astype(f32)
        return total

    def w_rows(zz, half):
        zz = (zz + 16) % 16
        span = rows(yl, 64) if half is None else rows(2 * yl + half, 32)
        return wb.at[zz % 4, zz // 4, span, :]

    def w_send(zz, off, half=None):
        return send(w_rows(zz, half), w_rows(zz, half), off)

    fetches = []
    for i, (src, dst) in enumerate(
        [
            (up_in, up), (dn_in, dn), (w_in, w_rows(z, None)), (ups_in, ups), (hid_in, hid),
            (dm_in, dm), (dv_in, dv), (um_in, um), (uv_in, uv),
        ]
    ):
        fetches.append(pltpu.make_async_copy(src, dst, local_sem.at[i]))
        fetches[-1].start()
    barrier = pltpu.get_barrier_semaphore()
    for off in PEERS:
        pl.semaphore_signal(barrier, inc=1, device_id=device(inverse(off)), device_id_type=MESH)
    fetches[0].wait()
    fetches[1].wait()
    sa[slot, :, 0:512] = stack_columns(up[...]).astype(bf16)
    sa[slot, :, 512:640] = jnp.concatenate([dn[...], jnp.zeros_like(dn[...])], axis=0).astype(bf16)
    pl.semaphore_wait(barrier, len(PEERS))

    far = far_send(sa)
    fetches[2].wait()
    pair_a = [w_send(z, Y_LO)]
    w_far = [w_send(z, PLUS4), w_send(z, MINUS4)]
    for copy in fetches[3:]:
        copy.wait()
    position = lax.broadcasted_iota(jnp.int32, (LEN, 1024), 0)
    for s in range(8):
        total = jnp.float32(0.0)
        for t in range(8):
            total = total + jnp.where(groups[t] == groups[s], rewards[t], jnp.float32(0.0))
        advantage = rewards[s] - total / GROUP
        weight = jnp.where(position < lengths[s], -advantage, jnp.float32(0.0))
        span = slice(LEN * s, LEN * s + LEN)
        g[span, :] = (weight * ups[span, :].astype(f32)).astype(bf16)
    far = far_relay(sa, far)
    gt[...] = jnp.transpose(g[...].astype(f32)).astype(bf16)
    arrive(far)
    for i in range(4):
        pair = jnp.concatenate([sa[2 * i].astype(f32), sa[2 * i + 1].astype(f32)], axis=0)
        block = rows(4 * (z % 4) + i, 16)
        f[block, 0:512] = jnp.concatenate([pair[0:8, 0:512], pair[16:24, 0:512]], 0).astype(bf16)
        f[block, 512:1024] = jnp.concatenate([pair[8:16, 0:512], pair[24:32, 0:512]], 0).astype(bf16)
        f[block, 1024:1152] = jnp.concatenate([pair[0:8, 512:], pair[16:24, 512:]], 0).astype(bf16)
    near = near_send(f)
    arrive(near)

    a[0:256, :] = dot(f[:, 1024:1152], hid[...], 1, 1).astype(bf16)
    a[256:512, :] = dot(f[:, 0:1024], gt[...], 1, 0).astype(bf16)
    j = 2 * x + c
    scattered = []
    for i, off in enumerate(X_CORE):
        to = 2 * ((x + off[2] + 4) % 4) + (c + off[4]) % 2
        scattered.append(send(a.at[rows(to, 64)], rx.at[i], off))
    arrive(w_far)
    w_far2 = [w_send(z - 4, PLUS4, 0), w_send(z + 4, MINUS4, 1)]
    w_near = [w_send(z + b, off) for b in (0, 4, -4) for off in (PLUS1, MINUS1)]
    pair_a += [w_send(z + b, Y_LO) for b in (4, -4)]
    arrive(scattered)
    total = a[rows(j, 64), :].astype(f32)
    for i in range(7):
        total = total + rx[i].astype(f32)
    sy[...] = total.astype(bf16)
    s = send(sy, ty, Y_HI)
    s.wait_recv()
    low[rows(j, 64), :] = (sy[...].astype(f32) + ty[...].astype(f32)).astype(bf16)
    gathered = [send(low.at[rows(j, 64)], low.at[rows(j, 64)], off) for off in X_CORE]
    arrive(w_far2)
    w_near_last = [w_send(z + 8, off) for off in (PLUS1, MINUS1)]
    pair_a.append(w_send(z + 8, Y_LO))
    arrive(gathered)

    cd[...] = (adapter_scale * dot(low[256:512, :], hid[...], 1, 0)).astype(bf16)
    near_d = near_parts(cd, nrd)
    cu[...] = (adapter_scale * dot(low[0:256, :], g[...], 1, 0)).astype(bf16)
    near_u = near_parts(cu, nru)
    arrive(w_near)
    w_near2 = []
    pair_b = []
    for b in (0, 4, -4):
        w_near2 += [w_send(z + 1 + b, MINUS1, 0), w_send(z - 1 + b, PLUS1, 1)]
        pair_a.append(w_send(z + 1 + b, Y_LO))
        pair_b.append(w_send(z - 1 + b, Y_LO))
    arrive(near_d)
    md[...] = near_sum(cd, nrd).reshape(8, 8, 128)
    far_d = far_parts(md, frd)
    arrive(near_u)
    total = near_sum(cu, nru)
    for i in range(8):
        mu[i] = stack_columns(total[8 * i : 8 * i + 8]).astype(bf16)
    far_u = far_parts(mu, fru)
    far_d = relay_parts(md, frd, hd, far_d)
    arrive(w_near_last)
    w_near2 += [w_send(z + 9, MINUS1, 0), w_send(z + 7, PLUS1, 1)]
    pair_a.append(w_send(z + 9, Y_LO))
    pair_b.append(w_send(z + 7, Y_LO))
    far_u = relay_parts(mu, fru, hu, far_u)
    arrive(far_d)
    fdn[...], fdm[...], fdv[...] = adam(dn[...], far_sum(md, frd), dm[...], dv[...])
    sd[slot] = fdn[...]
    far_d = far_send(sd)
    arrive(far_u)
    grad = spread_columns(far_sum(mu, fru))
    fup[...], fum[...], fuv[...] = adam(up[...], grad, um[...], uv[...])
    su[slot] = stack_columns(fup[...]).astype(bf16)
    far_u = far_send(su)
    far_d = far_relay(sd, far_d)
    arrive(w_near2)
    pair_b += [w_send(z + 2 + b, Y_LO) for b in (0, 4, -4, 8)]
    far_u = far_relay(su, far_u)

    flip = (z + c) % 2
    kept = [(z + flip) % 4, (z + flip + 2) % 4]
    sent_on = [(z + 1 - flip) % 4, (z + 3 - flip) % 4]

    def product(step):
        for group in (sent_on[step], kept[step]):
            total = dot(wb[group].reshape(512, 1024), gt[...], 1, 0).astype(bf16)
            pt[group] = total.reshape(4, 128, 256)
            if group is sent_on[step]:
                copy = send(pt.at[group], pr1.at[step], CORE)
        return copy

    def core_sum(step):
        q[step] = (pt[kept[step]].astype(f32) + pr1[step].astype(f32)).astype(bf16)
        return [
            send(q.at[step, (x + off[2] + 4) % 4], pr2.at[step, i], off)
            for i, off in enumerate(X_RING)
        ]

    arrive(pair_a)
    core_a = product(0)
    arrive(far_d)
    fd[rows(z % 4, 64), :] = sd[...].reshape(64, 128).astype(bf16)
    near_d = near_send(fd)
    arrive(far_u)
    for i in range(4):
        pair = jnp.concatenate([su[2 * i].astype(f32), su[2 * i + 1].astype(f32)], axis=0)
        block = rows(4 * (z % 4) + i, 16)
        fu[block, 0:512] = jnp.concatenate([pair[0:8], pair[16:24]], 0).astype(bf16)
        fu[block, 512:1024] = jnp.concatenate([pair[8:16], pair[24:32]], 0).astype(bf16)
    near_u = near_send(fu)
    arrive([core_a])
    x_parts = core_sum(0)

    k = 2 * x + yh
    arrive(near_d)
    nd[c, k] = jnp.transpose(fd[...].astype(f32)).astype(bf16)
    s = send(nd.at[c, k], nd.at[c, k], Y_HI)
    arrive(pair_b)
    core_b = product(1)
    s.wait_recv()
    spread = [send(nd.at[c, rows(x, 2)], nd.at[c, rows(x, 2)], off) for off in X_RING]
    arrive([core_b])
    x_parts += core_sum(1)
    arrive(spread)
    s = send(nd.at[c], nd.at[c], CORE)
    arrive(x_parts)
    for step in range(2):
        total = q[step, x].astype(f32)
        for i in range(3):
            total = total + pr2[step, i].astype(f32)
        r[step] = total
    mine = (kept[0] // 2 + yh) % 2
    rb[...] = r[1 - mine].astype(bf16)
    s_p = send(rb, pr3, Y_HI)
    own = adapter_scale * dot(low[256:512, :], f[:, 1024:1152], 0, 0)
    s_p.wait_recv()
    hig[...] = (jnp.transpose(r[mine] + pr3[...].astype(f32)) + own).astype(bf16)
    s.wait_recv()
    arrive(near_u)
    for copy in sent:
        copy.wait_send()


def exchange(*args):
    def out(shape, dtype):
        return jax.ShapeDtypeStruct(shape, dtype)

    vmem = pl.BlockSpec(memory_space=pltpu.VMEM)
    scratch = [
        ((256, 128), bf16), ((256, 1024), bf16), ((8, 128), f32), ((8, 1024), f32),
        ((8, 128), f32), ((8, 128), f32), ((8, 1024), f32), ((8, 1024), f32),
        ((256, 1024), bf16), ((1024, 256), bf16), ((8, 16, 640), bf16), ((256, 1152), bf16),
        ((512, 256), bf16), ((7, 64, 256), bf16), ((64, 256), bf16), ((64, 256), bf16),
        ((512, 256), bf16),
        ((256, 128), bf16), ((256, 1024), bf16), ((3, 64, 128), bf16), ((3, 64, 1024), bf16),
        ((8, 8, 128), f32), ((8, 16, 512), bf16), ((7, 8, 128), f32), ((7, 16, 512), bf16),
        ((2, 8, 128), f32), ((2, 16, 512), bf16),
        ((8, 8, 128), f32), ((8, 16, 512), bf16), ((256, 128), bf16),
        ((4, 4, 128, 256), bf16), ((2, 4, 128, 256), bf16), ((2, 4, 128, 256), bf16),
        ((2, 3, 128, 256), bf16), ((2, 128, 256), f32), ((128, 256), bf16), ((128, 256), bf16),
    ]
    return pl.pallas_call(
        exchange_kernel,
        name="exchange",
        out_shape=[
            out((4, 4, 128, 1024), bf16),
            out((2, 8, 128, 256), bf16),
            out((256, 1024), bf16),
            out((256, 128), bf16),
            out((8, 128), f32),
            out((8, 1024), f32),
            out((8, 128), f32),
            out((8, 128), f32),
            out((8, 1024), f32),
            out((8, 1024), f32),
        ],
        in_specs=[pl.BlockSpec(memory_space=pltpu.SMEM)] * 3
        + [pl.BlockSpec(memory_space=pltpu.HBM)] * 9,
        out_specs=[vmem] * 10,
        scratch_shapes=[pltpu.VMEM(shape, dtype) for shape, dtype in scratch]
        + [
            pltpu.SemaphoreType.DMA((MESSAGES,)),
            pltpu.SemaphoreType.DMA((MESSAGES,)),
            pltpu.SemaphoreType.DMA((9,)),
        ],
        compiler_params=pltpu.CompilerParams(
            collective_id=0, has_side_effects=True, vmem_limit_bytes=62 << 20
        ),
    )(*args)


def merge_kernel(w, nd, fu, *refs):
    merged = refs[-1]
    i = pl.program_id(0)
    factor = jnp.concatenate([nd[n % 2, 2 * i + n // 2] for n in range(4)], axis=0)
    delta = adapter_scale * dot(factor, fu[...], 1, 0)
    for n in range(4):
        span = slice(128 * n, 128 * n + 128)
        merged[span, :] = (w[n, i].astype(f32) + delta[span]).astype(bf16)

    @pl.when(i == 0)
    def _():
        for n in range(7):
            refs[7 + n][...] = refs[n][...]


def merge(w, nd, fu, *rest):
    vmem = pl.BlockSpec(memory_space=pltpu.VMEM)

    def whole(array):
        return pl.BlockSpec(array.shape, lambda i: (0,) * len(array.shape))

    return pl.pallas_call(
        merge_kernel,
        name="merge",
        grid=(4,),
        in_specs=[vmem] * 10,
        out_specs=[whole(array) for array in rest]
        + [pl.BlockSpec((512, 1024), lambda i: (i, 0))],
        out_shape=[jax.ShapeDtypeStruct(array.shape, array.dtype) for array in rest]
        + [jax.ShapeDtypeStruct((2048, 1024), bf16)],
        compiler_params=pltpu.CompilerParams(vmem_limit_bytes=62 << 20),
    )(w, nd, fu, *rest)


def body(
    hidden,
    upstream,
    rewards,
    groups,
    lengths,
    frozen_projection_weight,
    *adapter,
):
    w_all, nd, fu, *rest = exchange(
        rewards, groups, lengths, hidden, upstream, frozen_projection_weight, *adapter
    )
    return tuple(merge(w_all, nd, fu, *rest))


def solution(mesh):
    split = P("dp", "fsdp")
    in_specs = (split, split, P("dp"), P("dp"), P("dp")) + (split,) * 7
    out_specs = (split,) * 7 + (P(None, "fsdp"),)
    return jax.shard_map(body, mesh=mesh, in_specs=in_specs, out_specs=out_specs, check_vma=False)
```

```python
import jax
import jax.numpy as jnp
from jax import lax
from jax.experimental import pallas as pl
from jax.experimental.pallas import tpu as pltpu
from jax.sharding import PartitionSpec as P

GROUP = 4
LEN = 32
MESH = pl.DeviceIdType.MESH

adapter_scale = 2.0
learn_rate = 0.003
beta_one = 0.9
beta_two = 0.999
corr_one = 1.0 - 0.9**10
corr_two = 1.0 - 0.999**10
adam_eps = 1e-08

bf16 = jnp.bfloat16
f32 = jnp.float32

Y_LO = (0, 1, 0, 0, 0)
Y_HI = (0, 0, 0, 1, 0)
CORE = (0, 0, 0, 0, 1)
FAR = tuple((dz, dy, 0, 0, 0) for dz, dy in ((4, 0), (-4, 1), (4, 1), (-4, 0), (0, 1)))
PLUS4, MINUS4_ACROSS, _, MINUS4, _ = FAR
NEAR = tuple((dz, 0, 0, 0, 0) for dz in (2, -2, 1, -1))
PLUS2, MINUS2, PLUS1, MINUS1 = NEAR
X_RING = tuple((0, 0, dx, 0, 0) for dx in (2, 1, -1))
X_CORE = tuple((0, 0, dx, 0, dc) for dx in (2, 1, -1, 0) for dc in (1, 0) if (dx, dc) != (0, 0))
PEERS = FAR + NEAR + (Y_HI,) + X_CORE
MESSAGES = 128


def coords():
    dp = lax.axis_index("dp")
    fs = lax.axis_index("fsdp")
    return dp // 2, dp % 2, fs // 4, (fs // 2) % 2, fs % 2


def device(off):
    z, yl, x, yh, c = coords()
    z = (z + off[0] + 16) % 16
    yl = (yl + off[1]) % 2
    x = (x + off[2] + 4) % 4
    yh = (yh + off[3]) % 2
    c = (c + off[4]) % 2
    return (2 * z + yl, 4 * x + 2 * yh + c)


def inverse(off):
    return (-off[0], off[1], -off[2], off[3], off[4])


def dot(left, right, left_dim, right_dim):
    return lax.dot_general(
        left, right, (((left_dim,), (right_dim,)), ((), ())), preferred_element_type=f32
    )


def rows(start, size):
    return pl.ds(pl.multiple_of(start * size, size), size)


def adam(param, grad, mean, var):
    next_mean = beta_one * mean + (1.0 - beta_one) * grad
    next_var = beta_two * var + (1.0 - beta_two) * grad * grad
    update = next_mean / corr_one / (jnp.sqrt(next_var / corr_two) + adam_eps)
    return (param - learn_rate * update, next_mean, next_var)


def spread_columns(slot):
    return jnp.concatenate([slot[0:8], slot[8:16]], axis=1)


def stack_columns(block):
    half = block.shape[1] // 2
    return jnp.concatenate([block[:, :half], block[:, half:]], axis=0)


def exchange_kernel(
    rewards, groups, lengths, hid_in, ups_in, w_in, dn_in, up_in, dm_in, dv_in, um_in, uv_in,
    w_all, nd, fu, hig, fdn, fup, fdm, fdv, fum, fuv,
    hid, ups, dn, up, dm, dv, um, uv,
    wb, g, gt, sa, f, a, rx, sy, ty, low,
    cd, cu, nrd, nru, md, mu, frd, fru, hd, hu, sd, su, fd,
    pt, pr1, q, pr2, r, rb, pr3, send_sem, recv_sem, local_sem,
):
    z, yl, x, yh, c = coords()
    slot = 2 * (z // 4) + yl
    count = [0]
    sent = []

    def send(src, dst, off):
        i = count[0]
        count[0] += 1
        assert i < MESSAGES
        copy = pltpu.make_async_remote_copy(
            src_ref=src,
            dst_ref=dst,
            send_sem=send_sem.at[i],
            recv_sem=recv_sem.at[i],
            device_id=device(off),
            device_id_type=MESH,
        )
        copy.start()
        sent.append(copy)
        return copy

    def arrive(copies):
        for copy in copies:
            copy.wait_recv()

    def slot_of(dz, dy):
        return 2 * (((z + dz + 16) % 16) // 4) + (yl + dy) % 2

    def far_send(buf):
        return [send(buf.at[slot], buf.at[slot], off) for off in FAR]

    def far_relay(buf, copies):
        arrive(copies[:2])
        back, ahead = buf.at[slot_of(-4, 0)], buf.at[slot_of(4, 1)]
        return copies[2:] + [send(back, back, PLUS4), send(ahead, ahead, MINUS4)]

    def near_send(buf):
        mine = rows(z % 4, 64)
        low_half, high_half = rows(2 * (z % 4), 32), rows(2 * (z % 4) + 1, 32)
        return [
            send(buf.at[low_half], buf.at[low_half], PLUS2),
            send(buf.at[high_half], buf.at[high_half], MINUS2),
            send(buf.at[mine], buf.at[mine], PLUS1),
            send(buf.at[mine], buf.at[mine], MINUS1),
        ]

    def near_parts(buf, slots):
        across = (z + 2) % 4
        return [
            send(buf.at[rows(2 * across, 32)], slots.at[2, pl.ds(0, 32)], PLUS2),
            send(buf.at[rows(2 * across + 1, 32)], slots.at[2, pl.ds(32, 32)], MINUS2),
            send(buf.at[rows((z + 1) % 4, 64)], slots.at[0], PLUS1),
            send(buf.at[rows((z + 3) % 4, 64)], slots.at[1], MINUS1),
        ]

    def near_sum(buf, slots):
        total = buf[rows(z % 4, 64), :].astype(f32)
        for i in range(3):
            total = total + slots[i].astype(f32)
        return total

    def far_parts(buf, slots):
        relayed = [
            send(buf.at[slot_of(8, 0)], slots.at[5], PLUS4),
            send(buf.at[slot_of(8, 1)], slots.at[6], MINUS4),
        ]
        direct = [
            send(buf.at[slot_of(off[0], off[1])], slots.at[i], off)
            for i, off in enumerate(FAR)
            if i >= 2
        ]
        return relayed, direct

    def relay_parts(buf, slots, held, copies):
        relayed, direct = copies
        for i, off in enumerate(FAR[:2]):
            relayed[i].wait_recv()
            total = buf[slot_of(off[0], off[1])].astype(f32) + slots[5 + i].astype(f32)
            held[i] = total.astype(held.dtype)
            direct.append(send(held.at[i], slots.at[i], off))
        return direct

    def far_sum(buf, slots):
        total = buf[slot].astype(f32)
        for i in range(5):
            total = total + slots[i].astype(f32)
        return total

    def w_rows(zz, half):
        zz = (zz + 16) % 16
        span = rows(yl, 64) if half is None else rows(2 * yl + half, 32)
        return wb.at[zz % 4, zz // 4, span, :]

    def w_send(zz, off, half=None):
        return send(w_rows(zz, half), w_rows(zz, half), off)

    def w_step(step):
        arrive(w_ring)
        w_ring.clear()
        if step < 9:
            half = (0, 1) if step == 8 else (None, None)
            w_ring.extend(
                [w_send(z + 1 - step, PLUS1, half[0]), w_send(z - 1 + step, MINUS1, half[1])]
            )
        w_ready.extend([z] if step == 1 else [z + 8] if step == 9 else [z + 1 - step, z - 1 + step])
        if step != 4:
            w_pair.extend([w_send(zz, Y_LO) for zz in w_ready])
            w_ready.clear()

    w_ring = []
    w_ready = []
    w_pair = []
    fetches = []
    for i, (src, dst) in enumerate(
        [
            (up_in, up), (dn_in, dn), (w_in, w_rows(z, None)), (ups_in, ups), (hid_in, hid),
            (dm_in, dm), (dv_in, dv), (um_in, um), (uv_in, uv),
        ]
    ):
        fetches.append(pltpu.make_async_copy(src, dst, local_sem.at[i]))
        fetches[-1].start()
    flip = (z + c) % 2
    kept = [(z + flip) % 4, (z + flip + 2) % 4]
    sent_on = [(z + 1 - flip) % 4, (z + 3 - flip) % 4]

    def product(step):
        for group in (sent_on[step], kept[step]):
            total = dot(wb[group].reshape(512, 1024), gt[...], 1, 0).astype(bf16)
            pt[group] = total.reshape(4, 128, 256)
            if group is sent_on[step]:
                copy = send(pt.at[group], pr1.at[step], CORE)
        return copy

    def core_sum(step):
        q[step] = (pt[kept[step]].astype(f32) + pr1[step].astype(f32)).astype(bf16)
        return [
            send(q.at[step, (x + off[2] + 4) % 4], pr2.at[step, i], off)
            for i, off in enumerate(X_RING)
        ]


    barrier = pltpu.get_barrier_semaphore()
    for off in PEERS:
        pl.semaphore_signal(barrier, inc=1, device_id=device(inverse(off)), device_id_type=MESH)
    fetches[0].wait()
    fetches[1].wait()
    sa[slot, :, 0:512] = stack_columns(up[...]).astype(bf16)
    sa[slot, :, 512:640] = jnp.concatenate([dn[...], jnp.zeros_like(dn[...])], axis=0).astype(bf16)
    pl.semaphore_wait(barrier, len(PEERS))

    far = far_send(sa)
    fetches[2].wait()
    w_step(1)
    for copy in fetches[3:]:
        copy.wait()
    position = lax.broadcasted_iota(jnp.int32, (LEN, 1024), 0)
    for s in range(8):
        total = jnp.float32(0.0)
        for t in range(8):
            total = total + jnp.where(groups[t] == groups[s], rewards[t], jnp.float32(0.0))
        advantage = rewards[s] - total / GROUP
        weight = jnp.where(position < lengths[s], -advantage, jnp.float32(0.0))
        span = slice(LEN * s, LEN * s + LEN)
        g[span, :] = (weight * ups[span, :].astype(f32)).astype(bf16)
    far = far_relay(sa, far)
    gt[...] = jnp.transpose(g[...].astype(f32)).astype(bf16)
    arrive(far)
    for i in range(4):
        pair = jnp.concatenate([sa[2 * i].astype(f32), sa[2 * i + 1].astype(f32)], axis=0)
        block = rows(4 * (z % 4) + i, 16)
        f[block, 0:512] = jnp.concatenate([pair[0:8, 0:512], pair[16:24, 0:512]], 0).astype(bf16)
        f[block, 512:1024] = jnp.concatenate([pair[8:16, 0:512], pair[24:32, 0:512]], 0).astype(bf16)
        f[block, 1024:1152] = jnp.concatenate([pair[0:8, 512:], pair[16:24, 512:]], 0).astype(bf16)
    near = near_send(f)
    w_step(2)
    arrive(near)

    a[0:256, :] = dot(f[:, 1024:1152], hid[...], 1, 1).astype(bf16)
    a[256:512, :] = dot(f[:, 0:1024], gt[...], 1, 0).astype(bf16)
    j = 2 * x + c
    scattered = []
    for i, off in enumerate(X_CORE):
        to = 2 * ((x + off[2] + 4) % 4) + (c + off[4]) % 2
        scattered.append(send(a.at[rows(to, 64)], rx.at[i], off))
    w_step(3)
    arrive(scattered[:4])
    w_step(4)
    arrive(scattered[4:])
    total = a[rows(j, 64), :].astype(f32)
    for i in range(7):
        total = total + rx[i].astype(f32)
    sy[...] = total.astype(bf16)
    s = send(sy, ty, Y_HI)
    w_step(5)
    s.wait_recv()
    low[rows(j, 64), :] = (sy[...].astype(f32) + ty[...].astype(f32)).astype(bf16)
    gathered = [send(low.at[rows(j, 64)], low.at[rows(j, 64)], off) for off in X_CORE]
    w_step(6)
    arrive(gathered)

    cd[...] = (adapter_scale * dot(low[256:512, :], hid[...], 1, 0)).astype(bf16)
    near_d = near_parts(cd, nrd)
    cu[...] = (adapter_scale * dot(low[0:256, :], g[...], 1, 0)).astype(bf16)
    near_u = near_parts(cu, nru)
    w_step(7)
    arrive(near_d)
    md[...] = near_sum(cd, nrd).reshape(8, 8, 128)
    far_d = far_parts(md, frd)
    w_step(8)
    far_d = relay_parts(md, frd, hd, far_d)
    arrive(near_u)
    total = near_sum(cu, nru)
    for i in range(8):
        mu[i] = stack_columns(total[8 * i : 8 * i + 8]).astype(bf16)
    far_u = far_parts(mu, fru)
    w_step(9)
    arrive(far_d)
    fdn[...], fdm[...], fdv[...] = adam(dn[...], far_sum(md, frd), dm[...], dv[...])
    sd[slot] = fdn[...]
    far_d = far_send(sd)
    far_u = relay_parts(mu, fru, hu, far_u)
    far_d = far_relay(sd, far_d)
    arrive(far_u)
    grad = spread_columns(far_sum(mu, fru))
    fup[...], fum[...], fuv[...] = adam(up[...], grad, um[...], uv[...])
    su[slot] = stack_columns(fup[...]).astype(bf16)
    far_u = far_send(su)
    arrive(w_pair)
    w_copy = pltpu.make_async_copy(wb, w_all, local_sem.at[9])
    w_copy.start()
    core = [product(0), product(1)]
    arrive(far_d)
    fd[rows(z % 4, 64), :] = sd[...].reshape(64, 128).astype(bf16)
    near_d = near_send(fd)
    far_u = far_relay(su, far_u)
    arrive(core)
    x_parts = core_sum(0) + core_sum(1)

    k = 2 * x + yh
    arrive(near_d)
    nd[c, k] = jnp.transpose(fd[...].astype(f32)).astype(bf16)
    s = send(nd.at[c, k], nd.at[c, k], Y_HI)
    arrive(far_u)
    for i in range(4):
        pair = jnp.concatenate([su[2 * i].astype(f32), su[2 * i + 1].astype(f32)], axis=0)
        block = rows(4 * (z % 4) + i, 16)
        fu[block, 0:512] = jnp.concatenate([pair[0:8], pair[16:24]], 0).astype(bf16)
        fu[block, 512:1024] = jnp.concatenate([pair[8:16], pair[24:32]], 0).astype(bf16)
    near_u = near_send(fu)
    s.wait_recv()
    spread = [send(nd.at[c, rows(x, 2)], nd.at[c, rows(x, 2)], off) for off in X_RING]
    arrive(x_parts)
    for step in range(2):
        total = q[step, x].astype(f32)
        for i in range(3):
            total = total + pr2[step, i].astype(f32)
        r[step] = total
    mine = (kept[0] // 2 + yh) % 2
    rb[...] = r[1 - mine].astype(bf16)
    s_p = send(rb, pr3, Y_HI)
    own = adapter_scale * dot(low[256:512, :], f[:, 1024:1152], 0, 0)
    s_p.wait_recv()
    hig[...] = (jnp.transpose(r[mine] + pr3[...].astype(f32)) + own).astype(bf16)
    arrive(spread)
    s = send(nd.at[c], nd.at[c], CORE)
    s.wait_recv()
    arrive(near_u)
    for copy in sent:
        copy.wait_send()
    w_copy.wait()


def exchange(*args):
    def out(shape, dtype):
        return jax.ShapeDtypeStruct(shape, dtype)

    vmem = pl.BlockSpec(memory_space=pltpu.VMEM)
    scratch = [
        ((256, 128), bf16), ((256, 1024), bf16), ((8, 128), f32), ((8, 1024), f32),
        ((8, 128), f32), ((8, 128), f32), ((8, 1024), f32), ((8, 1024), f32),
        ((4, 4, 128, 1024), bf16),
        ((256, 1024), bf16), ((1024, 256), bf16), ((8, 16, 640), bf16), ((256, 1152), bf16),
        ((512, 256), bf16), ((7, 64, 256), bf16), ((64, 256), bf16), ((64, 256), bf16),
        ((512, 256), bf16),
        ((256, 128), bf16), ((256, 1024), bf16), ((3, 64, 128), bf16), ((3, 64, 1024), bf16),
        ((8, 8, 128), f32), ((8, 16, 512), bf16), ((7, 8, 128), f32), ((7, 16, 512), bf16),
        ((2, 8, 128), f32), ((2, 16, 512), bf16),
        ((8, 8, 128), f32), ((8, 16, 512), bf16), ((256, 128), bf16),
        ((4, 4, 128, 256), bf16), ((2, 4, 128, 256), bf16), ((2, 4, 128, 256), bf16),
        ((2, 3, 128, 256), bf16), ((2, 128, 256), f32), ((128, 256), bf16), ((128, 256), bf16),
    ]
    return pl.pallas_call(
        exchange_kernel,
        name="exchange",
        out_shape=[
            out((4, 4, 128, 1024), bf16),
            out((2, 8, 128, 256), bf16),
            out((256, 1024), bf16),
            out((256, 128), bf16),
            out((8, 128), f32),
            out((8, 1024), f32),
            out((8, 128), f32),
            out((8, 128), f32),
            out((8, 1024), f32),
            out((8, 1024), f32),
        ],
        in_specs=[pl.BlockSpec(memory_space=pltpu.SMEM)] * 3
        + [pl.BlockSpec(memory_space=pltpu.HBM)] * 9,
        out_specs=[pl.BlockSpec(memory_space=pltpu.HBM)] + [vmem] * 9,
        scratch_shapes=[pltpu.VMEM(shape, dtype) for shape, dtype in scratch]
        + [
            pltpu.SemaphoreType.DMA((MESSAGES,)),
            pltpu.SemaphoreType.DMA((MESSAGES,)),
            pltpu.SemaphoreType.DMA((10,)),
        ],
        compiler_params=pltpu.CompilerParams(
            collective_id=0, has_side_effects=True, vmem_limit_bytes=62 << 20
        ),
    )(*args)


def merge_kernel(w, nd, fu, *refs):
    merged = refs[-1]
    i = pl.program_id(0)
    blocks = [(n, half) for half in range(2) for n in range(4)]
    factor = jnp.concatenate([nd[n % 2, 2 * half + n // 2] for n, half in blocks], axis=0)
    delta = adapter_scale * dot(factor, fu[...], 1, 0)
    for at, (n, half) in enumerate(blocks):
        span = slice(128 * at, 128 * at + 128)
        merged[span, :] = (w[n, half].astype(f32) + delta[span]).astype(bf16)

    @pl.when(i == 0)
    def _():
        for n in range(7):
            refs[7 + n][...] = refs[n][...]


def merge(w, nd, fu, *rest):
    def whole(array):
        return pl.BlockSpec(array.shape, lambda i: (0,) * len(array.shape))

    return pl.pallas_call(
        merge_kernel,
        name="merge",
        grid=(2,),
        in_specs=[
            pl.BlockSpec((4, 2, 128, 1024), lambda i: (0, i, 0, 0)),
            pl.BlockSpec((2, 4, 128, 256), lambda i: (0, i, 0, 0)),
            whole(fu),
        ]
        + [whole(array) for array in rest],
        out_specs=[whole(array) for array in rest]
        + [pl.BlockSpec((1024, 1024), lambda i: (i, 0))],
        out_shape=[jax.ShapeDtypeStruct(array.shape, array.dtype) for array in rest]
        + [jax.ShapeDtypeStruct((2048, 1024), bf16)],
        compiler_params=pltpu.CompilerParams(vmem_limit_bytes=62 << 20),
    )(w, nd, fu, *rest)


def body(
    hidden,
    upstream,
    rewards,
    groups,
    lengths,
    frozen_projection_weight,
    *adapter,
):
    w_all, nd, fu, *rest = exchange(
        rewards, groups, lengths, hidden, upstream, frozen_projection_weight, *adapter
    )
    return tuple(merge(w_all, nd, fu, *rest))


def solution(mesh):
    split = P("dp", "fsdp")
    in_specs = (split, split, P("dp"), P("dp"), P("dp")) + (split,) * 7
    out_specs = (split,) * 7 + (P(None, "fsdp"),)
    return jax.shard_map(body, mesh=mesh, in_specs=in_specs, out_specs=out_specs, check_vma=False)
```

```python
import jax
import jax.numpy as jnp
from jax import lax
from jax.experimental import pallas as pl
from jax.experimental.pallas import tpu as pltpu
from jax.sharding import PartitionSpec as P

GROUP = 4
LEN = 32
MESH = pl.DeviceIdType.MESH

adapter_scale = 2.0
learn_rate = 0.003
beta_one = 0.9
beta_two = 0.999
corr_one = 1.0 - 0.9**10
corr_two = 1.0 - 0.999**10
adam_eps = 1e-08

bf16 = jnp.bfloat16
f32 = jnp.float32

Y_LO = (0, 1, 0, 0, 0)
Y_HI = (0, 0, 0, 1, 0)
CORE = (0, 0, 0, 0, 1)
FAR = tuple((dz, dy, 0, 0, 0) for dz, dy in ((4, 0), (-4, 1), (4, 1), (-4, 0), (0, 1)))
PLUS4, MINUS4_ACROSS, _, MINUS4, _ = FAR
NEAR = tuple((dz, 0, 0, 0, 0) for dz in (2, -2, 1, -1))
PLUS2, MINUS2, PLUS1, MINUS1 = NEAR
X_RING = tuple((0, 0, dx, 0, 0) for dx in (2, 1, -1))
X_CORE = tuple((0, 0, dx, 0, dc) for dx in (2, 1, -1, 0) for dc in (1, 0) if (dx, dc) != (0, 0))
PEERS = FAR + NEAR + (Y_HI,) + X_CORE
MESSAGES = 128


def coords():
    dp = lax.axis_index("dp")
    fs = lax.axis_index("fsdp")
    return dp // 2, dp % 2, fs // 4, (fs // 2) % 2, fs % 2


def device(off):
    z, yl, x, yh, c = coords()
    z = (z + off[0] + 16) % 16
    yl = (yl + off[1]) % 2
    x = (x + off[2] + 4) % 4
    yh = (yh + off[3]) % 2
    c = (c + off[4]) % 2
    return (2 * z + yl, 4 * x + 2 * yh + c)


def inverse(off):
    return (-off[0], off[1], -off[2], off[3], off[4])


def dot(left, right, left_dim, right_dim):
    return lax.dot_general(
        left, right, (((left_dim,), (right_dim,)), ((), ())), preferred_element_type=f32
    )


def rows(start, size):
    return pl.ds(pl.multiple_of(start * size, size), size)


def adam(param, grad, mean, var):
    next_mean = beta_one * mean + (1.0 - beta_one) * grad
    next_var = beta_two * var + (1.0 - beta_two) * grad * grad
    update = next_mean / corr_one / (jnp.sqrt(next_var / corr_two) + adam_eps)
    return (param - learn_rate * update, next_mean, next_var)


def spread_columns(slot):
    return jnp.concatenate([slot[0:8], slot[8:16]], axis=1)


def stack_columns(block):
    half = block.shape[1] // 2
    return jnp.concatenate([block[:, :half], block[:, half:]], axis=0)


def exchange_kernel(
    rewards, groups, lengths, hid_in, ups_in, w_in, dn_in, up_in, dm_in, dv_in, um_in, uv_in,
    w_all, nd, fu, hig, fdn, fup, fdm, fdv, fum, fuv,
    hid, ups, dn, up, dm, dv, um, uv,
    wb, g, gt, sa, f, a, rx, sy, ty, low,
    cd, cu, nrd, nru, md, mu, frd, fru, hd, hu, sd, su, fd,
    pt, pr1, q, pr2, r, rb, pr3, send_sem, recv_sem, local_sem,
):
    z, yl, x, yh, c = coords()
    slot = 2 * (z // 4) + yl
    count = [0]
    sent = []

    def send(src, dst, off):
        i = count[0]
        count[0] += 1
        assert i < MESSAGES
        copy = pltpu.make_async_remote_copy(
            src_ref=src,
            dst_ref=dst,
            send_sem=send_sem.at[i],
            recv_sem=recv_sem.at[i],
            device_id=device(off),
            device_id_type=MESH,
        )
        copy.start()
        sent.append(copy)
        return copy

    def arrive(copies):
        for copy in copies:
            copy.wait_recv()

    def slot_of(dz, dy):
        return 2 * (((z + dz + 16) % 16) // 4) + (yl + dy) % 2

    def far_send(buf):
        return [send(buf.at[slot], buf.at[slot], off) for off in FAR]

    def far_relay(buf, copies):
        arrive(copies[:2])
        back, ahead = buf.at[slot_of(-4, 0)], buf.at[slot_of(4, 1)]
        return copies[2:] + [send(back, back, PLUS4), send(ahead, ahead, MINUS4)]

    def near_send(buf):
        mine = rows(z % 4, 64)
        low_half, high_half = rows(2 * (z % 4), 32), rows(2 * (z % 4) + 1, 32)
        return [
            send(buf.at[low_half], buf.at[low_half], PLUS2),
            send(buf.at[high_half], buf.at[high_half], MINUS2),
            send(buf.at[mine], buf.at[mine], PLUS1),
            send(buf.at[mine], buf.at[mine], MINUS1),
        ]

    def near_parts(buf, slots):
        across = (z + 2) % 4
        return [
            send(buf.at[rows(2 * across, 32)], slots.at[2, pl.ds(0, 32)], PLUS2),
            send(buf.at[rows(2 * across + 1, 32)], slots.at[2, pl.ds(32, 32)], MINUS2),
            send(buf.at[rows((z + 1) % 4, 64)], slots.at[0], PLUS1),
            send(buf.at[rows((z + 3) % 4, 64)], slots.at[1], MINUS1),
        ]

    def near_sum(buf, slots):
        total = buf[rows(z % 4, 64), :].astype(f32)
        for i in range(3):
            total = total + slots[i].astype(f32)
        return total

    def far_parts(buf, slots):
        relayed = [
            send(buf.at[slot_of(8, 0)], slots.at[5], PLUS4),
            send(buf.at[slot_of(8, 1)], slots.at[6], MINUS4),
        ]
        direct = [
            send(buf.at[slot_of(off[0], off[1])], slots.at[i], off)
            for i, off in enumerate(FAR)
            if i >= 2
        ]
        return relayed, direct

    def relay_parts(buf, slots, held, copies):
        relayed, direct = copies
        for i, off in enumerate(FAR[:2]):
            relayed[i].wait_recv()
            total = buf[slot_of(off[0], off[1])].astype(f32) + slots[5 + i].astype(f32)
            held[i] = total.astype(held.dtype)
            direct.append(send(held.at[i], slots.at[i], off))
        return direct

    def far_sum(buf, slots):
        total = buf[slot].astype(f32)
        for i in range(5):
            total = total + slots[i].astype(f32)
        return total

    def w_rows(zz, half):
        zz = (zz + 16) % 16
        span = rows(yl, 64) if half is None else rows(2 * yl + half, 32)
        return wb.at[zz % 4, zz // 4, span, :]

    def w_send(zz, off, half=None):
        return send(w_rows(zz, half), w_rows(zz, half), off)

    def w_step(step):
        arrive(w_ring)
        w_ring.clear()
        if step < 9:
            half = (0, 1) if step == 8 else (None, None)
            w_ring.extend(
                [w_send(z + 1 - step, PLUS1, half[0]), w_send(z - 1 + step, MINUS1, half[1])]
            )
        w_ready.extend([z] if step == 1 else [z + 8] if step == 9 else [z + 1 - step, z - 1 + step])
        if step != 4:
            w_pair.extend([w_send(zz, Y_LO) for zz in w_ready])
            w_ready.clear()

    w_ring = []
    w_ready = []
    w_pair = []
    fetches = []
    for i, (src, dst) in enumerate(
        [
            (up_in, up), (dn_in, dn), (w_in, w_rows(z, None)), (ups_in, ups), (hid_in, hid),
            (dm_in, dm), (dv_in, dv), (um_in, um), (uv_in, uv),
        ]
    ):
        fetches.append(pltpu.make_async_copy(src, dst, local_sem.at[i]))
        fetches[-1].start()
    flip = (z + c) % 2
    kept = [(z + flip) % 4, (z + flip + 2) % 4]
    sent_on = [(z + 1 - flip) % 4, (z + 3 - flip) % 4]

    def product(step):
        for group in (sent_on[step], kept[step]):
            total = dot(wb[group].reshape(512, 1024), gt[...], 1, 0).astype(bf16)
            pt[group] = total.reshape(4, 128, 256)
            if group is sent_on[step]:
                copy = send(pt.at[group], pr1.at[step], CORE)
        return copy

    def core_sum(step):
        q[step] = (pt[kept[step]].astype(f32) + pr1[step].astype(f32)).astype(bf16)
        return [
            send(q.at[step, (x + off[2] + 4) % 4], pr2.at[step, i], off)
            for i, off in enumerate(X_RING)
        ]


    barrier = pltpu.get_barrier_semaphore()
    for off in PEERS:
        pl.semaphore_signal(barrier, inc=1, device_id=device(inverse(off)), device_id_type=MESH)
    fetches[0].wait()
    fetches[1].wait()
    sa[slot, :, 0:512] = stack_columns(up[...]).astype(bf16)
    sa[slot, :, 512:640] = jnp.concatenate([dn[...], jnp.zeros_like(dn[...])], axis=0).astype(bf16)
    pl.semaphore_wait(barrier, len(PEERS))

    far = far_send(sa)
    fetches[2].wait()
    w_step(1)
    for copy in fetches[3:]:
        copy.wait()
    position = lax.broadcasted_iota(jnp.int32, (LEN, 1024), 0)
    for s in range(8):
        total = jnp.float32(0.0)
        for t in range(8):
            total = total + jnp.where(groups[t] == groups[s], rewards[t], jnp.float32(0.0))
        advantage = rewards[s] - total / GROUP
        weight = jnp.where(position < lengths[s], -advantage, jnp.float32(0.0))
        span = slice(LEN * s, LEN * s + LEN)
        g[span, :] = (weight * ups[span, :].astype(f32)).astype(bf16)
    far = far_relay(sa, far)
    gt[...] = jnp.transpose(g[...].astype(f32)).astype(bf16)
    arrive(far)
    for i in range(4):
        pair = jnp.concatenate([sa[2 * i].astype(f32), sa[2 * i + 1].astype(f32)], axis=0)
        block = rows(4 * (z % 4) + i, 16)
        f[block, 0:512] = jnp.concatenate([pair[0:8, 0:512], pair[16:24, 0:512]], 0).astype(bf16)
        f[block, 512:1024] = jnp.concatenate([pair[8:16, 0:512], pair[24:32, 0:512]], 0).astype(bf16)
        f[block, 1024:1152] = jnp.concatenate([pair[0:8, 512:], pair[16:24, 512:]], 0).astype(bf16)
    near = near_send(f)
    w_step(2)
    arrive(near)

    a[0:256, :] = dot(f[:, 1024:1152], hid[...], 1, 1).astype(bf16)
    a[256:512, :] = dot(f[:, 0:1024], gt[...], 1, 0).astype(bf16)
    j = 2 * x + c
    scattered = []
    for i, off in enumerate(X_CORE):
        to = 2 * ((x + off[2] + 4) % 4) + (c + off[4]) % 2
        scattered.append(send(a.at[rows(to, 64)], rx.at[i], off))
    w_step(3)
    arrive(scattered[:4])
    w_step(4)
    arrive(scattered[4:])
    total = a[rows(j, 64), :].astype(f32)
    for i in range(7):
        total = total + rx[i].astype(f32)
    sy[...] = total.astype(bf16)
    s = send(sy, ty, Y_HI)
    w_step(5)
    s.wait_recv()
    low[rows(j, 64), :] = (sy[...].astype(f32) + ty[...].astype(f32)).astype(bf16)
    gathered = [send(low.at[rows(j, 64)], low.at[rows(j, 64)], off) for off in X_CORE]
    w_step(6)
    arrive(gathered)

    cd[...] = (adapter_scale * dot(low[256:512, :], hid[...], 1, 0)).astype(bf16)
    near_d = near_parts(cd, nrd)
    cu[...] = (adapter_scale * dot(low[0:256, :], g[...], 1, 0)).astype(bf16)
    near_u = near_parts(cu, nru)
    w_step(7)
    arrive(near_d)
    md[...] = near_sum(cd, nrd).reshape(8, 8, 128)
    far_d = far_parts(md, frd)
    far_d = relay_parts(md, frd, hd, far_d)
    arrive(near_u)
    total = near_sum(cu, nru)
    for i in range(8):
        mu[i] = stack_columns(total[8 * i : 8 * i + 8]).astype(bf16)
    far_u = far_parts(mu, fru)
    w_step(8)
    arrive(far_d)
    fdn[...], fdm[...], fdv[...] = adam(dn[...], far_sum(md, frd), dm[...], dv[...])
    sd[slot] = fdn[...]
    far_d = far_send(sd)
    far_u = relay_parts(mu, fru, hu, far_u)
    far_d = far_relay(sd, far_d)
    w_step(9)
    arrive(far_u)
    grad = spread_columns(far_sum(mu, fru))
    fup[...], fum[...], fuv[...] = adam(up[...], grad, um[...], uv[...])
    su[slot] = stack_columns(fup[...]).astype(bf16)
    far_u = far_send(su)
    arrive(w_pair)
    w_copy = pltpu.make_async_copy(wb, w_all, local_sem.at[9])
    w_copy.start()
    core = [product(0), product(1)]
    arrive(far_d)
    fd[rows(z % 4, 64), :] = sd[...].reshape(64, 128).astype(bf16)
    near_d = near_send(fd)
    far_u = far_relay(su, far_u)
    arrive(core)
    x_parts = core_sum(0) + core_sum(1)

    k = 2 * x + yh
    arrive(near_d)
    nd[c, k] = jnp.transpose(fd[...].astype(f32)).astype(bf16)
    s = send(nd.at[c, k], nd.at[c, k], Y_HI)
    arrive(far_u)
    for i in range(4):
        pair = jnp.concatenate([su[2 * i].astype(f32), su[2 * i + 1].astype(f32)], axis=0)
        block = rows(4 * (z % 4) + i, 16)
        fu[block, 0:512] = jnp.concatenate([pair[0:8], pair[16:24]], 0).astype(bf16)
        fu[block, 512:1024] = jnp.concatenate([pair[8:16], pair[24:32]], 0).astype(bf16)
    near_u = near_send(fu)
    s.wait_recv()
    block = nd.at[c, rows(x, 2)]
    spread = [send(block, block, off) for off in X_RING]
    across = [send(block, block, CORE)]
    arrive(x_parts)
    for step in range(2):
        total = q[step, x].astype(f32)
        for i in range(3):
            total = total + pr2[step, i].astype(f32)
        r[step] = total
    mine = (kept[0] // 2 + yh) % 2
    rb[...] = r[1 - mine].astype(bf16)
    s_p = send(rb, pr3, Y_HI)
    own = adapter_scale * dot(low[256:512, :], f[:, 1024:1152], 0, 0)
    for i in (1, 2, 0):
        arrive([spread[i]])
        block = nd.at[c, rows((x - X_RING[i][2] + 4) % 4, 2)]
        across.append(send(block, block, CORE))
    s_p.wait_recv()
    hig[...] = (jnp.transpose(r[mine] + pr3[...].astype(f32)) + own).astype(bf16)
    arrive(across)
    arrive(near_u)
    for copy in sent:
        copy.wait_send()
    w_copy.wait()


def exchange(*args):
    def out(shape, dtype):
        return jax.ShapeDtypeStruct(shape, dtype)

    vmem = pl.BlockSpec(memory_space=pltpu.VMEM)
    scratch = [
        ((256, 128), bf16), ((256, 1024), bf16), ((8, 128), f32), ((8, 1024), f32),
        ((8, 128), f32), ((8, 128), f32), ((8, 1024), f32), ((8, 1024), f32),
        ((4, 4, 128, 1024), bf16),
        ((256, 1024), bf16), ((1024, 256), bf16), ((8, 16, 640), bf16), ((256, 1152), bf16),
        ((512, 256), bf16), ((7, 64, 256), bf16), ((64, 256), bf16), ((64, 256), bf16),
        ((512, 256), bf16),
        ((256, 128), bf16), ((256, 1024), bf16), ((3, 64, 128), bf16), ((3, 64, 1024), bf16),
        ((8, 8, 128), f32), ((8, 16, 512), bf16), ((7, 8, 128), f32), ((7, 16, 512), bf16),
        ((2, 8, 128), f32), ((2, 16, 512), bf16),
        ((8, 8, 128), f32), ((8, 16, 512), bf16), ((256, 128), bf16),
        ((4, 4, 128, 256), bf16), ((2, 4, 128, 256), bf16), ((2, 4, 128, 256), bf16),
        ((2, 3, 128, 256), bf16), ((2, 128, 256), f32), ((128, 256), bf16), ((128, 256), bf16),
    ]
    return pl.pallas_call(
        exchange_kernel,
        name="exchange",
        out_shape=[
            out((4, 4, 128, 1024), bf16),
            out((2, 8, 128, 256), bf16),
            out((256, 1024), bf16),
            out((256, 128), bf16),
            out((8, 128), f32),
            out((8, 1024), f32),
            out((8, 128), f32),
            out((8, 128), f32),
            out((8, 1024), f32),
            out((8, 1024), f32),
        ],
        in_specs=[pl.BlockSpec(memory_space=pltpu.SMEM)] * 3
        + [pl.BlockSpec(memory_space=pltpu.HBM)] * 9,
        out_specs=[pl.BlockSpec(memory_space=pltpu.HBM)] + [vmem] * 9,
        scratch_shapes=[pltpu.VMEM(shape, dtype) for shape, dtype in scratch]
        + [
            pltpu.SemaphoreType.DMA((MESSAGES,)),
            pltpu.SemaphoreType.DMA((MESSAGES,)),
            pltpu.SemaphoreType.DMA((10,)),
        ],
        compiler_params=pltpu.CompilerParams(
            collective_id=0, has_side_effects=True, vmem_limit_bytes=62 << 20
        ),
    )(*args)


def merge_kernel(w, nd, fu, *refs):
    merged = refs[-1]
    i = pl.program_id(0)
    blocks = [(n, half) for half in range(2) for n in range(4)]
    factor = jnp.concatenate([nd[n % 2, 2 * half + n // 2] for n, half in blocks], axis=0)
    delta = adapter_scale * dot(factor, fu[...], 1, 0)
    for at, (n, half) in enumerate(blocks):
        span = slice(128 * at, 128 * at + 128)
        merged[span, :] = (w[n, half].astype(f32) + delta[span]).astype(bf16)

    @pl.when(i == 0)
    def _():
        for n in range(7):
            refs[7 + n][...] = refs[n][...]


def merge(w, nd, fu, *rest):
    def whole(array):
        return pl.BlockSpec(array.shape, lambda i: (0,) * len(array.shape))

    return pl.pallas_call(
        merge_kernel,
        name="merge",
        grid=(2,),
        in_specs=[
            pl.BlockSpec((4, 2, 128, 1024), lambda i: (0, i, 0, 0)),
            pl.BlockSpec((2, 4, 128, 256), lambda i: (0, i, 0, 0)),
            whole(fu),
        ]
        + [whole(array) for array in rest],
        out_specs=[whole(array) for array in rest]
        + [pl.BlockSpec((1024, 1024), lambda i: (i, 0))],
        out_shape=[jax.ShapeDtypeStruct(array.shape, array.dtype) for array in rest]
        + [jax.ShapeDtypeStruct((2048, 1024), bf16)],
        compiler_params=pltpu.CompilerParams(vmem_limit_bytes=62 << 20),
    )(w, nd, fu, *rest)


def body(
    hidden,
    upstream,
    rewards,
    groups,
    lengths,
    frozen_projection_weight,
    *adapter,
):
    w_all, nd, fu, *rest = exchange(
        rewards, groups, lengths, hidden, upstream, frozen_projection_weight, *adapter
    )
    return tuple(merge(w_all, nd, fu, *rest))


def solution(mesh):
    split = P("dp", "fsdp")
    in_specs = (split, split, P("dp"), P("dp"), P("dp")) + (split,) * 7
    out_specs = (split,) * 7 + (P(None, "fsdp"),)
    return jax.shard_map(body, mesh=mesh, in_specs=in_specs, out_specs=out_specs, check_vma=False)
```

```python
import jax
import jax.numpy as jnp
from jax import lax
from jax.experimental import pallas as pl
from jax.experimental.pallas import tpu as pltpu
from jax.sharding import PartitionSpec as P

GROUP = 4
LEN = 32
MESH = pl.DeviceIdType.MESH

adapter_scale = 2.0
learn_rate = 0.003
beta_one = 0.9
beta_two = 0.999
corr_one = 1.0 - 0.9**10
corr_two = 1.0 - 0.999**10
adam_eps = 1e-08

bf16 = jnp.bfloat16
f32 = jnp.float32

Y_LO = (0, 1, 0, 0, 0)
Y_HI = (0, 0, 0, 1, 0)
CORE = (0, 0, 0, 0, 1)
FAR = tuple((dz, dy, 0, 0, 0) for dz, dy in ((4, 0), (-4, 1), (4, 1), (-4, 0), (0, 1)))
PLUS4, MINUS4_ACROSS, _, MINUS4, _ = FAR
NEAR = tuple((dz, 0, 0, 0, 0) for dz in (2, -2, 1, -1))
PLUS2, MINUS2, PLUS1, MINUS1 = NEAR
X_RING = tuple((0, 0, dx, 0, 0) for dx in (2, 1, -1))
X_CORE = tuple((0, 0, dx, 0, dc) for dx in (2, 1, -1, 0) for dc in (1, 0) if (dx, dc) != (0, 0))
PEERS = FAR + NEAR + (Y_HI,) + X_CORE
MESSAGES = 128


def coords():
    dp = lax.axis_index("dp")
    fs = lax.axis_index("fsdp")
    return dp // 2, dp % 2, fs // 4, (fs // 2) % 2, fs % 2


def device(off):
    z, yl, x, yh, c = coords()
    z = (z + off[0] + 16) % 16
    yl = (yl + off[1]) % 2
    x = (x + off[2] + 4) % 4
    yh = (yh + off[3]) % 2
    c = (c + off[4]) % 2
    return (2 * z + yl, 4 * x + 2 * yh + c)


def inverse(off):
    return (-off[0], off[1], -off[2], off[3], off[4])


def dot(left, right, left_dim, right_dim):
    return lax.dot_general(
        left, right, (((left_dim,), (right_dim,)), ((), ())), preferred_element_type=f32
    )


def rows(start, size):
    return pl.ds(pl.multiple_of(start * size, size), size)


def adam(param, grad, mean, var):
    next_mean = beta_one * mean + (1.0 - beta_one) * grad
    next_var = beta_two * var + (1.0 - beta_two) * grad * grad
    update = next_mean / corr_one / (jnp.sqrt(next_var / corr_two) + adam_eps)
    return (param - learn_rate * update, next_mean, next_var)


def spread_columns(slot):
    return jnp.concatenate([slot[0:8], slot[8:16]], axis=1)


def stack_columns(block):
    half = block.shape[1] // 2
    return jnp.concatenate([block[:, :half], block[:, half:]], axis=0)


def exchange_kernel(
    rewards, groups, lengths, hid_in, ups_in, w_in, dn_in, up_in, dm_in, dv_in, um_in, uv_in,
    w_all, nd, fu, hig, fdn, fup, fdm, fdv, fum, fuv,
    hid, ups, dn, up, dm, dv, um, uv,
    wb, g, gt, sa, f, a, rx, sy, ty, low,
    cd, cu, nrd, nru, md, mu, frd, fru, hd, hu, sd, su, fd,
    pt, pr1, q, pr2, r, rb, pr3, send_sem, recv_sem, local_sem,
):
    z, yl, x, yh, c = coords()
    slot = 2 * (z // 4) + yl
    count = [0]
    sent = []

    def send(src, dst, off):
        i = count[0]
        count[0] += 1
        assert i < MESSAGES
        copy = pltpu.make_async_remote_copy(
            src_ref=src,
            dst_ref=dst,
            send_sem=send_sem.at[i],
            recv_sem=recv_sem.at[i],
            device_id=device(off),
            device_id_type=MESH,
        )
        copy.start()
        sent.append(copy)
        return copy

    def arrive(copies):
        for copy in copies:
            copy.wait_recv()

    def slot_of(dz, dy):
        return 2 * (((z + dz + 16) % 16) // 4) + (yl + dy) % 2

    def far_send(buf):
        return [send(buf.at[slot], buf.at[slot], off) for off in FAR]

    def far_relay(buf, copies):
        arrive(copies[:2])
        back, ahead = buf.at[slot_of(-4, 0)], buf.at[slot_of(4, 1)]
        return copies[2:] + [send(back, back, PLUS4), send(ahead, ahead, MINUS4)]

    def near_send(buf):
        mine = rows(z % 4, 64)
        low_half, high_half = rows(2 * (z % 4), 32), rows(2 * (z % 4) + 1, 32)
        return [
            send(buf.at[low_half], buf.at[low_half], PLUS2),
            send(buf.at[high_half], buf.at[high_half], MINUS2),
            send(buf.at[mine], buf.at[mine], PLUS1),
            send(buf.at[mine], buf.at[mine], MINUS1),
        ]

    def near_parts(buf, slots):
        across = (z + 2) % 4
        return [
            send(buf.at[rows(2 * across, 32)], slots.at[2, pl.ds(0, 32)], PLUS2),
            send(buf.at[rows(2 * across + 1, 32)], slots.at[2, pl.ds(32, 32)], MINUS2),
            send(buf.at[rows((z + 1) % 4, 64)], slots.at[0], PLUS1),
            send(buf.at[rows((z + 3) % 4, 64)], slots.at[1], MINUS1),
        ]

    def near_sum(buf, slots):
        total = buf[rows(z % 4, 64), :].astype(f32)
        for i in range(3):
            total = total + slots[i].astype(f32)
        return total

    def far_parts(buf, slots):
        relayed = [
            send(buf.at[slot_of(8, 0)], slots.at[5], PLUS4),
            send(buf.at[slot_of(8, 1)], slots.at[6], MINUS4),
        ]
        direct = [
            send(buf.at[slot_of(off[0], off[1])], slots.at[i], off)
            for i, off in enumerate(FAR)
            if i >= 2
        ]
        return relayed, direct

    def relay_parts(buf, slots, held, copies):
        relayed, direct = copies
        for i, off in enumerate(FAR[:2]):
            relayed[i].wait_recv()
            total = buf[slot_of(off[0], off[1])].astype(f32) + slots[5 + i].astype(f32)
            held[i] = total.astype(held.dtype)
            direct.append(send(held.at[i], slots.at[i], off))
        return direct

    def far_sum(buf, slots):
        total = buf[slot].astype(f32)
        for i in range(5):
            total = total + slots[i].astype(f32)
        return total

    def w_rows(zz, half):
        zz = (zz + 16) % 16
        span = rows(yl, 64) if half is None else rows(2 * yl + half, 32)
        return wb.at[zz % 4, zz // 4, span, :]

    def w_send(zz, off, half=None):
        return send(w_rows(zz, half), w_rows(zz, half), off)

    def w_step(step):
        arrive(w_ring)
        w_ring.clear()
        if step < 9:
            half = (0, 1) if step == 8 else (None, None)
            w_ring.extend(
                [w_send(z + 1 - step, PLUS1, half[0]), w_send(z - 1 + step, MINUS1, half[1])]
            )
        w_ready.extend([z] if step == 1 else [z + 8] if step == 9 else [z + 1 - step, z - 1 + step])
        w_pair.extend([w_send(zz, Y_LO) for zz in w_ready])
        w_ready.clear()

    w_ring = []
    w_ready = []
    w_pair = []
    fetches = []
    for i, (src, dst) in enumerate(
        [
            (up_in, up), (dn_in, dn), (w_in, w_rows(z, None)), (ups_in, ups), (hid_in, hid),
            (dm_in, dm), (dv_in, dv), (um_in, um), (uv_in, uv),
        ]
    ):
        fetches.append(pltpu.make_async_copy(src, dst, local_sem.at[i]))
        fetches[-1].start()
    flip = (z + c) % 2
    kept = [(z + flip) % 4, (z + flip + 2) % 4]
    sent_on = [(z + 1 - flip) % 4, (z + 3 - flip) % 4]

    def product(step):
        for group in (sent_on[step], kept[step]):
            total = dot(wb[group].reshape(512, 1024), gt[...], 1, 0).astype(bf16)
            pt[group] = total.reshape(4, 128, 256)
            if group is sent_on[step]:
                copy = send(pt.at[group], pr1.at[step], CORE)
        return copy

    def core_sum(step):
        q[step] = (pt[kept[step]].astype(f32) + pr1[step].astype(f32)).astype(bf16)
        return [
            send(q.at[step, (x + off[2] + 4) % 4], pr2.at[step, i], off)
            for i, off in enumerate(X_RING)
        ]


    barrier = pltpu.get_barrier_semaphore()
    for off in PEERS:
        pl.semaphore_signal(barrier, inc=1, device_id=device(inverse(off)), device_id_type=MESH)
    fetches[0].wait()
    fetches[1].wait()
    sa[slot, :, 0:512] = stack_columns(up[...]).astype(bf16)
    sa[slot, :, 512:640] = jnp.concatenate([dn[...], jnp.zeros_like(dn[...])], axis=0).astype(bf16)
    pl.semaphore_wait(barrier, len(PEERS))

    far = far_send(sa)
    fetches[2].wait()
    w_step(1)
    for copy in fetches[3:]:
        copy.wait()
    position = lax.broadcasted_iota(jnp.int32, (LEN, 1024), 0)
    for s in range(8):
        total = jnp.float32(0.0)
        for t in range(8):
            total = total + jnp.where(groups[t] == groups[s], rewards[t], jnp.float32(0.0))
        advantage = rewards[s] - total / GROUP
        weight = jnp.where(position < lengths[s], -advantage, jnp.float32(0.0))
        span = slice(LEN * s, LEN * s + LEN)
        g[span, :] = (weight * ups[span, :].astype(f32)).astype(bf16)
    far = far_relay(sa, far)
    gt[...] = jnp.transpose(g[...].astype(f32)).astype(bf16)
    w_step(2)
    arrive(far)
    for i in range(4):
        pair = jnp.concatenate([sa[2 * i].astype(f32), sa[2 * i + 1].astype(f32)], axis=0)
        block = rows(4 * (z % 4) + i, 16)
        f[block, 0:512] = jnp.concatenate([pair[0:8, 0:512], pair[16:24, 0:512]], 0).astype(bf16)
        f[block, 512:1024] = jnp.concatenate([pair[8:16, 0:512], pair[24:32, 0:512]], 0).astype(bf16)
        f[block, 1024:1152] = jnp.concatenate([pair[0:8, 512:], pair[16:24, 512:]], 0).astype(bf16)
    near = near_send(f)
    w_step(3)
    arrive(near)

    a[0:256, :] = dot(f[:, 1024:1152], hid[...], 1, 1).astype(bf16)
    a[256:512, :] = dot(f[:, 0:1024], gt[...], 1, 0).astype(bf16)
    j = 2 * x + c
    scattered = []
    for i, off in enumerate(X_CORE):
        to = 2 * ((x + off[2] + 4) % 4) + (c + off[4]) % 2
        scattered.append(send(a.at[rows(to, 64)], rx.at[i], off))
    w_step(4)
    arrive(scattered)
    total = a[rows(j, 64), :].astype(f32)
    for i in range(7):
        total = total + rx[i].astype(f32)
    sy[...] = total.astype(bf16)
    s = send(sy, ty, Y_HI)
    w_step(5)
    s.wait_recv()
    low[rows(j, 64), :] = (sy[...].astype(f32) + ty[...].astype(f32)).astype(bf16)
    gathered = [send(low.at[rows(j, 64)], low.at[rows(j, 64)], off) for off in X_CORE]
    w_step(6)
    arrive(gathered)

    cd[...] = (adapter_scale * dot(low[256:512, :], hid[...], 1, 0)).astype(bf16)
    near_d = near_parts(cd, nrd)
    cu[...] = (adapter_scale * dot(low[0:256, :], g[...], 1, 0)).astype(bf16)
    near_u = near_parts(cu, nru)
    w_step(7)
    arrive(near_d)
    md[...] = near_sum(cd, nrd).reshape(8, 8, 128)
    far_d = far_parts(md, frd)
    far_d = relay_parts(md, frd, hd, far_d)
    arrive(near_u)
    total = near_sum(cu, nru)
    for i in range(8):
        mu[i] = stack_columns(total[8 * i : 8 * i + 8]).astype(bf16)
    far_u = far_parts(mu, fru)
    w_step(8)
    arrive(far_d)
    fdn[...], fdm[...], fdv[...] = adam(dn[...], far_sum(md, frd), dm[...], dv[...])
    sd[slot] = fdn[...]
    far_d = far_send(sd)
    far_u = relay_parts(mu, fru, hu, far_u)
    far_d = far_relay(sd, far_d)
    w_step(9)
    arrive(far_u)
    grad = spread_columns(far_sum(mu, fru))
    fup[...], fum[...], fuv[...] = adam(up[...], grad, um[...], uv[...])
    su[slot] = stack_columns(fup[...]).astype(bf16)
    far_u = far_send(su)
    arrive(w_pair)
    w_copy = pltpu.make_async_copy(wb, w_all, local_sem.at[9])
    w_copy.start()
    core = [product(0), product(1)]
    arrive(far_d)
    fd[rows(z % 4, 64), :] = sd[...].reshape(64, 128).astype(bf16)
    near_d = near_send(fd)
    far_u = far_relay(su, far_u)
    arrive(core)
    x_parts = core_sum(0) + core_sum(1)

    k = 2 * x + yh
    arrive(near_d)
    nd[c, k] = jnp.transpose(fd[...].astype(f32)).astype(bf16)
    s = send(nd.at[c, k], nd.at[c, k], Y_HI)
    arrive(far_u)
    for i in range(4):
        pair = jnp.concatenate([su[2 * i].astype(f32), su[2 * i + 1].astype(f32)], axis=0)
        block = rows(4 * (z % 4) + i, 16)
        fu[block, 0:512] = jnp.concatenate([pair[0:8], pair[16:24]], 0).astype(bf16)
        fu[block, 512:1024] = jnp.concatenate([pair[8:16], pair[24:32]], 0).astype(bf16)
    near_u = near_send(fu)
    s.wait_recv()
    block = nd.at[c, rows(x, 2)]
    spread = [send(block, block, off) for off in X_RING]
    across = [send(block, block, CORE)]
    arrive(x_parts)
    for step in range(2):
        total = q[step, x].astype(f32)
        for i in range(3):
            total = total + pr2[step, i].astype(f32)
        r[step] = total
    mine = (kept[0] // 2 + yh) % 2
    rb[...] = r[1 - mine].astype(bf16)
    s_p = send(rb, pr3, Y_HI)
    own = adapter_scale * dot(low[256:512, :], f[:, 1024:1152], 0, 0)
    for i in (1, 2, 0):
        arrive([spread[i]])
        block = nd.at[c, rows((x - X_RING[i][2] + 4) % 4, 2)]
        across.append(send(block, block, CORE))
    s_p.wait_recv()
    hig[...] = (jnp.transpose(r[mine] + pr3[...].astype(f32)) + own).astype(bf16)
    arrive(across)
    arrive(near_u)
    for copy in sent:
        copy.wait_send()
    w_copy.wait()


def exchange(*args):
    def out(shape, dtype):
        return jax.ShapeDtypeStruct(shape, dtype)

    vmem = pl.BlockSpec(memory_space=pltpu.VMEM)
    scratch = [
        ((256, 128), bf16), ((256, 1024), bf16), ((8, 128), f32), ((8, 1024), f32),
        ((8, 128), f32), ((8, 128), f32), ((8, 1024), f32), ((8, 1024), f32),
        ((4, 4, 128, 1024), bf16),
        ((256, 1024), bf16), ((1024, 256), bf16), ((8, 16, 640), bf16), ((256, 1152), bf16),
        ((512, 256), bf16), ((7, 64, 256), bf16), ((64, 256), bf16), ((64, 256), bf16),
        ((512, 256), bf16),
        ((256, 128), bf16), ((256, 1024), bf16), ((3, 64, 128), bf16), ((3, 64, 1024), bf16),
        ((8, 8, 128), f32), ((8, 16, 512), bf16), ((7, 8, 128), f32), ((7, 16, 512), bf16),
        ((2, 8, 128), f32), ((2, 16, 512), bf16),
        ((8, 8, 128), f32), ((8, 16, 512), bf16), ((256, 128), bf16),
        ((4, 4, 128, 256), bf16), ((2, 4, 128, 256), bf16), ((2, 4, 128, 256), bf16),
        ((2, 3, 128, 256), bf16), ((2, 128, 256), f32), ((128, 256), bf16), ((128, 256), bf16),
    ]
    return pl.pallas_call(
        exchange_kernel,
        name="exchange",
        out_shape=[
            out((4, 4, 128, 1024), bf16),
            out((2, 8, 128, 256), bf16),
            out((256, 1024), bf16),
            out((256, 128), bf16),
            out((8, 128), f32),
            out((8, 1024), f32),
            out((8, 128), f32),
            out((8, 128), f32),
            out((8, 1024), f32),
            out((8, 1024), f32),
        ],
        in_specs=[pl.BlockSpec(memory_space=pltpu.SMEM)] * 3
        + [pl.BlockSpec(memory_space=pltpu.HBM)] * 9,
        out_specs=[pl.BlockSpec(memory_space=pltpu.HBM)] + [vmem] * 9,
        scratch_shapes=[pltpu.VMEM(shape, dtype) for shape, dtype in scratch]
        + [
            pltpu.SemaphoreType.DMA((MESSAGES,)),
            pltpu.SemaphoreType.DMA((MESSAGES,)),
            pltpu.SemaphoreType.DMA((10,)),
        ],
        compiler_params=pltpu.CompilerParams(
            collective_id=0, has_side_effects=True, vmem_limit_bytes=62 << 20
        ),
    )(*args)


def merge_kernel(w, nd, fu, *refs):
    merged = refs[-1]
    i = pl.program_id(0)
    blocks = [(n, half) for half in range(2) for n in range(4)]
    factor = jnp.concatenate([nd[n % 2, 2 * half + n // 2] for n, half in blocks], axis=0)
    delta = adapter_scale * dot(factor, fu[...], 1, 0)
    for at, (n, half) in enumerate(blocks):
        span = slice(128 * at, 128 * at + 128)
        merged[span, :] = (w[n, half].astype(f32) + delta[span]).astype(bf16)

    @pl.when(i == 0)
    def _():
        for n in range(7):
            refs[7 + n][...] = refs[n][...]


def merge(w, nd, fu, *rest):
    def whole(array):
        return pl.BlockSpec(array.shape, lambda i: (0,) * len(array.shape))

    return pl.pallas_call(
        merge_kernel,
        name="merge",
        grid=(2,),
        in_specs=[
            pl.BlockSpec((4, 2, 128, 1024), lambda i: (0, i, 0, 0)),
            pl.BlockSpec((2, 4, 128, 256), lambda i: (0, i, 0, 0)),
            whole(fu),
        ]
        + [whole(array) for array in rest],
        out_specs=[whole(array) for array in rest]
        + [pl.BlockSpec((1024, 1024), lambda i: (i, 0))],
        out_shape=[jax.ShapeDtypeStruct(array.shape, array.dtype) for array in rest]
        + [jax.ShapeDtypeStruct((2048, 1024), bf16)],
        compiler_params=pltpu.CompilerParams(vmem_limit_bytes=62 << 20),
    )(w, nd, fu, *rest)


def body(
    hidden,
    upstream,
    rewards,
    groups,
    lengths,
    frozen_projection_weight,
    *adapter,
):
    w_all, nd, fu, *rest = exchange(
        rewards, groups, lengths, hidden, upstream, frozen_projection_weight, *adapter
    )
    return tuple(merge(w_all, nd, fu, *rest))


def solution(mesh):
    split = P("dp", "fsdp")
    in_specs = (split, split, P("dp"), P("dp"), P("dp")) + (split,) * 7
    out_specs = (split,) * 7 + (P(None, "fsdp"),)
    return jax.shard_map(body, mesh=mesh, in_specs=in_specs, out_specs=out_specs, check_vma=False)
```
